512 devices in a mesh: queue: 64 (over z, x_lo, core), row: 8 (over x_hi, y).
Axes of the slice: x: 4 (x_hi: 2, x_lo: 2; x = x_hi * 2 + x_lo), y: 4, z: 16, core: 2. Of those that a mesh axis runs over, the one named last changes fastest.
Arguments:
- latents: float32 [64, 4, 8, 128], P('queue', None, 'row'), may hold values from -6 to 6
- fresh_noise: float32 [2, 4, 8, 128], P(None, None, 'row'), may hold values from -6 to 6
- timesteps: int32 [64, 2], P('queue'), may hold values from 0 to 899, as said below
- conv_in_w: bfloat16 [36, 320], replicated, may hold values from -1 to 1
- time_w: bfloat16 [320, 320], replicated, may hold values from -0.3125 to 0.3125
- spatial_in: bfloat16 [320, 960], replicated, may hold values from -3 to 3
- spatial_out: bfloat16 [320, 320], replicated, may hold values from -1.25 to 1.25
- temporal_in: bfloat16 [320, 960], replicated, may hold values from -3 to 3
- temporal_out: bfloat16 [320, 320], replicated, may hold values from -0.3125 to 0.3125
- conv_out_w: bfloat16 [320, 36], replicated, may hold values from -0.109375 to 0.109375
Outputs:
- denoised: float32 [2, 64, 4, 8, 128], P(None, 'queue', None, 'row')
- queue_out: float32 [64, 4, 8, 128], P('queue', None, 'row')
The draws below stay inside these ranges and needn't reach their ends.
Inputs may be any that keep to these rules, and one draw needn't show every extreme that they name: timesteps[k, 1] < timesteps[k, 0]; slot 0's target level is 0 and slot 63 starts at level 899.
All inputs are finite; a program needn't handle non-finite values.
Results may differ from the reference program's by a relative error of at most 0.0055.
Values may be sent and summed in bfloat16 or wider, within the bound.
A program may use at most 64 MiB of HBM per device.

```python
import math
import jax
import jax.numpy as jnp
from jax import lax

CH = 320
HEADS = 5
WIDTH = 128
ROWS = 8
QUEUE = 64
HALF = 4
STEPS = 2


def draw_latents(key, part):
    key = jax.random.fold_in(key, 11)
    second = jax.random.fold_in(key, 1)
    values = jax.random.normal(second, (QUEUE, 4, ROWS, WIDTH), jnp.float32)
    return jnp.clip(values, -6.0, 6.0)


def projection(key, strength):
    first, second, third = jax.random.split(key, 3)
    scale = CH ** (-0.5)
    query = jnp.clip(jax.random.normal(first, (CH, CH), jnp.float32), -5.0, 5.0)
    other = jnp.clip(jax.random.normal(second, (CH, CH), jnp.float32), -5.0, 5.0)
    value = jnp.clip(jax.random.normal(third, (CH, CH), jnp.float32), -5.0, 5.0)
    column = jnp.repeat(strength, CH // HEADS)
    keyed = other
    whole = jnp.concatenate([query * column, keyed * column, value], axis=1) * scale
    return jnp.clip(whole, -3.0, 3.0).astype(jnp.bfloat16)


def draw_spatial_in(key, part):
    key = jax.random.fold_in(key, 21)
    first = jax.random.fold_in(key, 0)
    strength = jnp.ones((HEADS,), jnp.float32)
    return projection(first, strength)


def draw_temporal_in(key, part):
    key = jax.random.fold_in(key, 41)
    first = jax.random.fold_in(key, 0)
    strength = jnp.ones((HEADS,), jnp.float32)
    return projection(first, strength)


def draw_timesteps(key, part):
    key = jax.random.fold_in(key, 31)
    first, second = jax.random.split(key)
    current = jax.random.randint(first, (QUEUE,), 100, 900, jnp.int32)
    current = current.at[QUEUE - 1].set(899)
    gap = jax.random.randint(second, (QUEUE,), 1, 100, jnp.int32)
    target = current - gap
    target = target.at[0].set(0)
    return jnp.stack([current, target], axis=1).astype(jnp.int32)


def steps_of(own_key, shape, cuts, low, high):
    loudness = 1.0
    for position, parts in cuts:
        draws = jax.random.uniform(jax.random.fold_in(jax.random.fold_in(own_key, 6), position), (parts,), jnp.float32, low / len(cuts), high / len(cuts))
        loudness = loudness * jnp.repeat(jnp.exp(draws), shape[position] // parts).reshape((-1,) + (1,) * (len(shape) - 1 - position))
    return loudness


def noise(rng, extent, scale, bound, cuts=(), held_as=jnp.bfloat16):
    loudness = steps_of(rng, extent, cuts, -0.22, 0.18) if cuts else 1.0
    array = jax.random.normal(rng, extent, jnp.float32) * scale * loudness
    return jnp.minimum(jnp.maximum(array, -bound), bound).astype(held_as)


def setup_inputs(seed: int = 0) -> dict:
    splits = jax.random.split(jax.random.key(seed), 11)
    return {
        "latents": draw_latents(jax.random.fold_in(splits[10], 71), 0),
        "fresh_noise": noise(splits[1], (STEPS, 4, ROWS, WIDTH), 1.0, 6.0, ((2, 8),), jnp.float32),
        "timesteps": draw_timesteps(jax.random.fold_in(splits[10], 71), 0),
        "conv_in_w": noise(splits[3], (36, CH), 36 ** -0.5, 1.0),
        "time_w": noise(splits[4], (CH, CH), CH ** -0.5, 0.3125),
        "spatial_in": draw_spatial_in(jax.random.fold_in(splits[10], 71), 0),
        "spatial_out": noise(splits[6], (CH, CH), (CH // 16) ** -0.5, 1.25),
        "temporal_in": draw_temporal_in(jax.random.fold_in(splits[10], 71), 0),
        "temporal_out": noise(splits[8], (CH, CH), CH ** -0.5, 0.3125),
        "conv_out_w": noise(splits[9], (CH, 36), (9 * CH) ** -0.5, 0.109375),
    }


def layer_norm(values):
    centre = values - lax.optimization_barrier(jnp.mean(values, axis=-1, keepdims=True))
    return centre * lax.rsqrt(lax.optimization_barrier(jnp.mean(centre * centre, axis=-1, keepdims=True)) + 1e-05)

def plan(level):
    start = 0.008 / 1.008 * math.pi / 2.0
    base = math.cos(start) ** 2
    angle = ((level + 1.0) / 1000.0 + 0.008) / 1.008 * (math.pi / 2.0)
    signal = jnp.cos(angle) ** 2 / base
    remain = jnp.sin(angle - start) * jnp.sin(angle + start) / base
    return (signal, remain)

def sinusoid(level, count):
    half_count = count // 2
    freqs = jnp.exp(-math.log(10000.0) * jnp.arange(half_count, dtype=jnp.float32) / half_count)
    angle = level * freqs
    return jnp.concatenate([jnp.cos(angle), jnp.sin(angle)], axis=-1)

def patches_of(padded, row_count, col_count):
    pieces = []
    for row_step in range(3):
        for col_step in range(3):
            pieces.append(padded[:, row_step:row_step + row_count, col_step:col_step + col_count])
    stacked = jnp.stack(pieces, 0)
    return jnp.transpose(stacked, (2, 3, 0, 1)).reshape(row_count * col_count, 36)

def tap_sum(taps, row_count, col_count):
    total = None
    for row_step in range(3):
        for col_step in range(3):
            tap_index = 3 * row_step + col_step
            term = taps[..., row_step:row_step + row_count, col_step:col_step + col_count, 4 * tap_index:4 * tap_index + 4]
            total = term if total is None else total + term
    return total

def reference(latents, fresh_noise, timesteps, conv_in_w, time_w, spatial_in, spatial_out, temporal_in, temporal_out, conv_out_w):
    queue_len = latents.shape[0]
    row_count = latents.shape[2]
    col_count = latents.shape[3]
    channels = conv_in_w.shape[1]
    head_dim = channels // HEADS
    pixels = row_count * col_count
    scale = 1.0 / math.sqrt(head_dim)
    level_now = timesteps[:, 0].astype(jnp.float32)
    level_next = timesteps[:, 1].astype(jnp.float32)
    signal_now, rest_now = plan(level_now)
    signal_next, rest_next = plan(level_next)
    signal_now = signal_now.reshape(queue_len, 1, 1, 1)
    rest_now = rest_now.reshape(queue_len, 1, 1, 1)
    signal_next = signal_next.reshape(queue_len, 1, 1, 1)
    rest_next = rest_next.reshape(queue_len, 1, 1, 1)
    span = 2 * HALF + 1
    offsets = jnp.arange(span, dtype=jnp.int32) - HALF
    target = jnp.arange(queue_len, dtype=jnp.int32)[None, :] + offsets[:, None]
    valid = (target >= 0) & (target < queue_len)

    def front(inputs):
        frame, level = inputs
        padded = jnp.pad(frame.astype(jnp.bfloat16), ((0, 0), (1, 1), (1, 1)))
        embedding = sinusoid(level, channels).astype(jnp.bfloat16)
        time_bias = jax.nn.silu(jnp.dot(embedding[None, :], time_w, preferred_element_type=jnp.float32))
        hidden = jnp.dot(patches_of(padded, row_count, col_count), conv_in_w, preferred_element_type=jnp.float32) + time_bias
        normed = layer_norm(hidden).astype(jnp.bfloat16)
        projected = jnp.dot(normed, spatial_in, preferred_element_type=jnp.float32).astype(jnp.bfloat16)
        queries = projected[:, :channels].reshape(pixels, HEADS, head_dim).astype(jnp.float32)
        keys = projected[:, channels:2 * channels].reshape(pixels, HEADS, head_dim).astype(jnp.float32)
        values = projected[:, 2 * channels:].reshape(pixels, HEADS, head_dim).astype(jnp.float32)
        scores = jnp.einsum('phd,rhd->hpr', queries, keys) * scale
        peak = lax.optimization_barrier(jnp.max(scores, axis=-1, keepdims=True))
        weights = jnp.exp(scores - peak)
        total = lax.optimization_barrier(jnp.sum(weights, axis=-1))
        rounded = weights.astype(jnp.bfloat16).astype(jnp.float32)
        blended = jnp.einsum('hpr,rhd->phd', rounded, values) / jnp.transpose(total)[:, :, None]
        mixed = blended.reshape(pixels, channels).astype(jnp.bfloat16)
        return hidden + jnp.dot(mixed, spatial_out, preferred_element_type=jnp.float32)
    state = latents
    outputs = []
    for step_index in range(STEPS):
        hidden = lax.map(front, (state, level_now))
        normed = layer_norm(hidden).astype(jnp.bfloat16)
        projected = jnp.dot(normed.reshape(queue_len * pixels, channels), temporal_in, preferred_element_type=jnp.float32).astype(jnp.bfloat16)
        projected = projected.reshape(queue_len, pixels, 3 * channels)
        queries = projected[..., :channels].reshape(queue_len, pixels, HEADS, head_dim).astype(jnp.float32)
        padded = jnp.pad(projected[..., channels:], ((HALF, HALF), (0, 0), (0, 0)))
        score_list = []
        for index in range(span):
            keys = padded[index:index + queue_len, :, :channels].reshape(queue_len, pixels, HEADS, head_dim).astype(jnp.float32)
            score_list.append(lax.optimization_barrier(jnp.sum(queries * keys, axis=-1)) * scale)
        scores = jnp.stack(score_list, 0)
        scores = jnp.where(valid[:, :, None, None], scores, -jnp.inf)
        peak = lax.optimization_barrier(jnp.max(scores, axis=0))
        weights = jnp.exp(scores - peak[None])
        total = lax.optimization_barrier(jnp.sum(weights, axis=0))
        rounded = weights.astype(jnp.bfloat16).astype(jnp.float32)
        blended = jnp.zeros((queue_len, pixels, HEADS, head_dim), jnp.float32)
        for index in range(span):
            values = padded[index:index + queue_len, :, channels:].reshape(queue_len, pixels, HEADS, head_dim).astype(jnp.float32)
            blended = blended + rounded[index][..., None] * values
        blended = blended / total[..., None]
        mixed = blended.reshape(queue_len * pixels, channels).astype(jnp.bfloat16)
        hidden = hidden + jnp.dot(mixed, temporal_out, preferred_element_type=jnp.float32).reshape(queue_len, pixels, channels)
        normed = layer_norm(hidden).astype(jnp.bfloat16).reshape(queue_len, row_count, col_count, channels)
        taps = jnp.dot(normed, conv_out_w, preferred_element_type=jnp.float32)
        taps = jnp.pad(taps, ((0, 0), (1, 1), (1, 1), (0, 0)))
        predicted = jnp.transpose(tap_sum(taps, row_count, col_count), (0, 3, 1, 2))
        clean = (state - jnp.sqrt(rest_now) * predicted) / jnp.sqrt(signal_now)
        fresh = jnp.sqrt(signal_next) * clean + jnp.sqrt(rest_next) * predicted
        outputs.append(fresh)
        state = jnp.concatenate([fresh[1:], fresh_noise[step_index][None]], axis=0)
    return (jnp.stack(outputs, 0), state)
```

```python
import functools
import math

import jax
import jax.numpy as jnp
from jax import lax
from jax.experimental import pallas as pl
from jax.experimental.pallas import tpu as pltpu
from jax.sharding import PartitionSpec as P

HEADS = 5
HALF = 4
STEPS = 2
SPAN = 2 * HALF + 1
F32 = jnp.float32
BF16 = jnp.bfloat16
MESH = pl.DeviceIdType.MESH
OFFSETS = (1, -1, 2, -2, 3, -3, 4, -4)


def dot(left, right):
    return jnp.dot(left, right, preferred_element_type=F32)


def dot_rows(left, right):
    return lax.dot_general(left, right, (((1,), (1,)), ((), ())), preferred_element_type=F32)


def dot_columns(left, right):
    return lax.dot_general(left, right, (((0,), (0,)), ((), ())), preferred_element_type=F32)


def plan(level):
    start = 0.008 / 1.008 * math.pi / 2.0
    base = math.cos(start) ** 2
    angle = ((level + 1.0) / 1000.0 + 0.008) / 1.008 * (math.pi / 2.0)
    signal = jnp.cos(angle) ** 2 / base
    remain = jnp.sin(angle - start) * jnp.sin(angle + start) / base
    return (signal, remain)


def shifted(tile, step):
    if step == 1:
        return tile
    width = tile.shape[1]
    lane = lax.broadcasted_iota(jnp.int32, tile.shape, 1)
    if step == 0:
        return jnp.where(lane == 0, 0.0, pltpu.roll(tile, 1, 1))
    return jnp.where(lane == width - 1, 0.0, pltpu.roll(tile, width - 1, 1))


def layer_norm_columns(values):
    centre = values - jnp.mean(values, axis=0, keepdims=True)
    return centre * lax.rsqrt(jnp.mean(centre * centre, axis=0, keepdims=True) + 1e-05)


def kernel(
    sizes,
    steps_ref,
    latents_ref,
    noise_ref,
    conv_in_hbm,
    time_hbm,
    spatial_in_hbm,
    spatial_out_hbm,
    temporal_in_hbm,
    temporal_out_hbm,
    conv_out_hbm,
    denoised_ref,
    queue_ref,
    conv_in_ref,
    time_ref,
    spatial_in_ref,
    spatial_out_ref,
    temporal_in_ref,
    temporal_out_ref,
    conv_out_ref,
    conv_in_t,
    spatial_in_t,
    spatial_out_t,
    temporal_in_t,
    temporal_out_t,
    conv_out_t,
    frame_ref,
    patch_ref,
    normed_ref,
    key_ref,
    value_ref,
    score_ref,
    weight_ref,
    tkv_ref,
    rows_ref,
    sent_ref,
    beside_ref,
    parts_ref,
    own_out_ref,
    next_out_ref,
    own_in_ref,
    load_sem,
    rows_send,
    rows_recv,
    beside_send,
    beside_recv,
    next_send,
    next_recv,
    own_send,
    own_recv,
):
    queue_len, row_len, comm = sizes
    channels = time_ref.shape[0]
    head_dim = channels // HEADS
    width = latents_ref.shape[3]
    pixels = row_len * width
    if comm:
        me_q = lax.axis_index("queue")
        me_r = lax.axis_index("row")
    else:
        me_q = 5
        me_r = 3

    def queue_at(offset):
        return lax.rem(me_q + offset + queue_len, queue_len)

    def row_at(offset):
        return lax.rem(me_r + offset + row_len, row_len)

    loads = [
        pltpu.make_async_copy(source, target, load_sem.at[index])
        for index, (source, target) in enumerate(
            (
                (time_hbm, time_ref),
                (conv_in_hbm, conv_in_ref),
                (spatial_in_hbm, spatial_in_ref),
                (spatial_out_hbm, spatial_out_ref),
                (temporal_in_hbm, temporal_in_ref),
                (temporal_out_hbm, temporal_out_ref),
                (conv_out_hbm, conv_out_ref),
            )
        )
    ]
    for load in loads:
        load.start()

    if comm:
        barrier = pltpu.get_barrier_semaphore()
        for offset in range(1, row_len):
            for q in (0, 1, -1):
                pl.semaphore_signal(
                    barrier, inc=1, device_id=(queue_at(q), row_at(offset)), device_id_type=MESH
                )
        for offset in OFFSETS:
            pl.semaphore_signal(
                barrier, inc=1, device_id=(queue_at(offset), me_r), device_id_type=MESH
            )

    latents = latents_ref[0, :, 0, :]
    empty = jnp.zeros_like(latents)
    rows_ref[me_r] = jnp.concatenate([latents, empty], axis=0)

    level_now = steps_ref[0, 0].astype(F32)
    level_next = steps_ref[0, 1].astype(F32)
    signal_now, rest_now = plan(jnp.full((8, width), level_now, F32))
    signal_next, rest_next = plan(jnp.full((8, width), level_next, F32))
    keep = jnp.sqrt(signal_next) / jnp.sqrt(signal_now)
    push = jnp.sqrt(rest_next) - keep * jnp.sqrt(rest_now)

    half = channels // 2
    column = lax.broadcasted_iota(jnp.int32, (8, channels), 1)
    place = jnp.where(column < half, column, column - half).astype(F32)
    angle = level_now * jnp.exp(place * (-math.log(10000.0) / half))
    embedding = jnp.where(column < half, jnp.cos(angle), jnp.sin(angle)).astype(BF16)
    loads[0].wait()
    projected = dot(embedding, time_ref[...])
    bias = projected[0:1] / (1.0 + jnp.exp(-projected[0:1]))
    bias = bias - jnp.mean(bias, axis=1, keepdims=True)

    loads[1].wait()
    wide = conv_in_ref[...].astype(F32)
    wide = wide - jnp.mean(wide, axis=1, keepdims=True)
    gap = jnp.zeros((4, channels), F32)
    pieces = []
    for row_step in range(3):
        for col_step in range(3):
            base = 4 * (3 * row_step + col_step)
            pieces.append(wide[base : base + 4])
            if row_step == 1 and col_step == 1:
                pieces.append(jnp.concatenate([bias, gap[0:3]], axis=0))
            else:
                pieces.append(gap)
        pieces.append(gap)
        pieces.append(gap)
    centred = jnp.concatenate(pieces, axis=0)
    high = centred.astype(BF16).astype(F32)
    low = centred - high
    conv_in_t[...] = jnp.concatenate([high, low], axis=0).T.astype(BF16)

    if comm:
        pl.semaphore_wait(barrier, 3 * (row_len - 1) + 2 * HALF)

    row_copies = []
    if comm:
        for offset in range(1, row_len):
            copy = pltpu.make_async_remote_copy(
                src_ref=rows_ref.at[me_r],
                dst_ref=rows_ref.at[me_r],
                send_sem=rows_send.at[offset],
                recv_sem=rows_recv.at[offset],
                device_id=(me_q, row_at(offset)),
                device_id_type=MESH,
            )
            copy.start()
            row_copies.append(copy)

    loads[2].wait()
    spatial_in_t[...] = spatial_in_ref[...].T
    loads[3].wait()
    spatial_out_t[...] = spatial_out_ref[...].T
    loads[4].wait()
    temporal_in_t[...] = temporal_in_ref[...].T
    loads[5].wait()
    temporal_out_t[...] = temporal_out_ref[...].T
    loads[6].wait()
    turned = conv_out_ref[...].astype(F32).T
    gap = jnp.zeros((4, channels), F32)
    pieces = []
    for col_step in range(3):
        for row_step in range(3):
            base = 4 * (3 * row_step + col_step)
            pieces.append(turned[base : base + 4])
            pieces.append(gap)
    pieces.append(jnp.zeros((8, channels), F32))
    conv_out_t[...] = jnp.concatenate(pieces, axis=0).astype(BF16)
    for head in range(HEADS):
        value_ref[head, head_dim : head_dim + 16, :] = jnp.ones((16, pixels), BF16)

    for copy in row_copies:
        copy.wait()

    own_columns = pl.ds(pl.multiple_of(me_r * width, width), width)
    sublane = lax.broadcasted_iota(jnp.int32, (8, width), 0)
    source_ref = rows_ref

    for step in range(STEPS):
        tiles = []
        for y in range(row_len):
            tile = source_ref[y]
            middle = jnp.where(sublane == 4, 1.0, tile)
            tiles.append(
                jnp.concatenate(
                    [shifted(tile, 0), middle, shifted(tile, 2), jnp.zeros_like(tile)], axis=0
                ).astype(BF16)
            )
        nothing = jnp.zeros_like(tiles[0])
        for y in range(row_len):
            for a in range(3):
                other = y + a - 1
                tile = tiles[other] if 0 <= other < row_len else nothing
                for part in range(2):
                    patch_ref[
                        96 * part + 32 * a : 96 * part + 32 * a + 32, y * width : (y + 1) * width
                    ] = tile
        state = source_ref[me_r]

        chunk = 2 * width
        for lower in range(0, pixels, chunk):
            span = slice(lower, lower + chunk)
            hidden = dot(conv_in_t[...], patch_ref[:, span])
            normed = (
                hidden * lax.rsqrt(jnp.mean(hidden * hidden, axis=0, keepdims=True) + 1e-05)
            ).astype(BF16)
            normed_ref[:, span] = normed
            pairs = dot(spatial_in_t[channels:, :], normed).astype(BF16)
            key_ref[:, span] = pairs[:channels]
            for head in range(HEADS):
                first = channels + head * head_dim
                value_ref[head, 0:head_dim, span] = pairs[first : first + head_dim]

        hidden = dot(conv_in_t[...], patch_ref[:, own_columns])
        queries = dot(spatial_in_t[:channels, :], normed_ref[:, own_columns]).astype(BF16) * (
            1.0 / math.sqrt(head_dim)
        )
        queries = queries.astype(BF16)

        mixed = []
        for head in range(HEADS):
            first = head * head_dim
            score_ref[head] = dot_columns(
                queries[first : first + head_dim], key_ref[first : first + head_dim, :]
            )
            for lower in range(0, width, 32):
                block = score_ref[head, lower : lower + 32, :]
                peak = jnp.max(block, axis=1, keepdims=True)
                weight_ref[head, lower : lower + 32, :] = jnp.exp(block - peak).astype(BF16)
            summed = dot_rows(value_ref[head], weight_ref[head])
            mixed.append(summed[0:head_dim] / summed[head_dim : head_dim + 1])
        mixed = jnp.concatenate(mixed, axis=0).astype(BF16)
        hidden = hidden + dot(spatial_out_t[...], mixed)
        normed = layer_norm_columns(hidden).astype(BF16)
        sent_ref[step] = normed

        copies = []
        if comm:
            for index, offset in enumerate(OFFSETS):
                copy = pltpu.make_async_remote_copy(
                    src_ref=sent_ref.at[step],
                    dst_ref=beside_ref.at[step, index],
                    send_sem=beside_send.at[step, index],
                    recv_sem=beside_recv.at[step, index],
                    device_id=(queue_at(offset), me_r),
                    device_id_type=MESH,
                )
                copy.start()
                copies.append(copy)

        projected = dot(temporal_in_t[...], normed).astype(BF16).astype(F32)
        tqueries = projected[:channels] * (1.0 / math.sqrt(head_dim))
        tkv_ref[2 * HALF] = projected[2 * channels :]
        scores = []

        def score_of(keys):
            return jnp.concatenate(
                [
                    jnp.sum(
                        tqueries[h * head_dim : (h + 1) * head_dim]
                        * keys[h * head_dim : (h + 1) * head_dim],
                        axis=0,
                        keepdims=True,
                    )
                    for h in range(HEADS)
                ],
                axis=0,
            )

        own_score = score_of(projected[channels : 2 * channels])
        for index in range(0, 2 * HALF, 2):
            for copy in copies[index : index + 2]:
                copy.wait_recv()
            both = jnp.concatenate([beside_ref[step, index], beside_ref[step, index + 1]], axis=1)
            projected = dot(temporal_in_t[channels:, :], both).astype(BF16).astype(F32)
            for inner in range(2):
                part = projected[:, inner * width : (inner + 1) * width]
                target = me_q - OFFSETS[index + inner]
                valid = jnp.logical_and(target >= 0, target < queue_len)
                scores.append(jnp.where(valid, score_of(part[:channels]), -jnp.inf))
                tkv_ref[index + inner] = part[channels:]
        scores.append(own_score)
        peak = functools.reduce(jnp.maximum, scores)
        weights = [jnp.exp(score - peak) for score in scores]
        total = functools.reduce(jnp.add, weights)
        rounded = [weight.astype(BF16).astype(F32) for weight in weights]
        mixed = []
        for head in range(HEADS):
            blended = None
            for index in range(SPAN):
                term = (
                    rounded[index][head : head + 1]
                    * tkv_ref[index, head * head_dim : (head + 1) * head_dim, :]
                )
                blended = term if blended is None else blended + term
            mixed.append(blended / total[head : head + 1])
        mixed = jnp.concatenate(mixed, axis=0).astype(BF16)
        hidden = hidden + dot(temporal_out_t[...], mixed)
        normed = layer_norm_columns(hidden).astype(BF16)

        taps = dot(conv_out_t[...], normed)
        added = shifted(taps[0:24], 0) + taps[24:48] + shifted(taps[48:72], 2)
        below = push * added[0:8]
        middle = push * added[8:16] + keep * state
        above = push * added[16:24]
        own_out_ref[step, 0] = below
        own_out_ref[step, 1] = above
        noise = jnp.concatenate([noise_ref[step, :, 0, :], empty], axis=0)
        entering = me_q == 0
        nothing = jnp.zeros_like(below)
        next_out_ref[step, 0:8] = jnp.where(entering, nothing, below)
        next_out_ref[step, 8:16] = jnp.where(entering, noise, middle)
        next_out_ref[step, 16:24] = jnp.where(entering, nothing, above)

        next_copies = []
        own_copies = []
        if comm:
            last = step == STEPS - 1
            offsets = (0, 1, row_len - 1) if last else range(row_len)
            for offset in offsets:
                copy = pltpu.make_async_remote_copy(
                    src_ref=next_out_ref.at[step],
                    dst_ref=parts_ref.at[step, me_r],
                    send_sem=next_send.at[step, offset],
                    recv_sem=next_recv.at[step, offset],
                    device_id=(queue_at(-1), row_at(offset)),
                    device_id_type=MESH,
                )
                copy.start()
                next_copies.append(copy)
            for slot, offset in enumerate((1, -1)):
                copy = pltpu.make_async_remote_copy(
                    src_ref=own_out_ref.at[step, slot],
                    dst_ref=own_in_ref.at[step, slot],
                    send_sem=own_send.at[step, slot],
                    recv_sem=own_recv.at[step, slot],
                    device_id=(me_q, row_at(offset)),
                    device_id_type=MESH,
                )
                copy.start()
                own_copies.append(copy)
        for copy in copies:
            copy.wait_send()
        for copy in next_copies:
            copy.wait()
        top_row = me_r == 0
        bottom_row = me_r == row_len - 1
        if step < STEPS - 1:
            for y in range(row_len):
                total = parts_ref[step, y, 8:16]
                if y > 0:
                    total = total + parts_ref[step, y - 1, 0:8]
                if y < row_len - 1:
                    total = total + parts_ref[step, y + 1, 16:24]
                frame_ref[y] = total
            source_ref = frame_ref
        else:
            total = parts_ref[step, me_r, 8:16]
            total = total + jnp.where(top_row, 0.0, parts_ref[step, row_at(-1), 0:8])
            total = total + jnp.where(bottom_row, 0.0, parts_ref[step, row_at(1), 16:24])
            queue_ref[0, :, 0, :] = total[0:4]
        for copy in own_copies:
            copy.wait()
        total = middle
        total = total + jnp.where(top_row, 0.0, own_in_ref[step, 0])
        total = total + jnp.where(bottom_row, 0.0, own_in_ref[step, 1])
        denoised_ref[step, 0, :, 0, :] = total[0:4]


def on_device(
    latents,
    fresh_noise,
    timesteps,
    conv_in_w,
    time_w,
    spatial_in,
    spatial_out,
    temporal_in,
    temporal_out,
    conv_out_w,
    *,
    sizes,
):
    queue_len, row_len, comm = sizes
    channels = conv_in_w.shape[1]
    head_dim = channels // HEADS
    width = latents.shape[3]
    pixels = row_len * width
    vmem = pl.BlockSpec(memory_space=pltpu.VMEM)
    hbm = pl.BlockSpec(memory_space=pl.ANY)
    dma = pltpu.SemaphoreType.DMA
    weights = (conv_in_w, time_w, spatial_in, spatial_out, temporal_in, temporal_out, conv_out_w)
    return pl.pallas_call(
        functools.partial(kernel, sizes),
        out_shape=(
            jax.ShapeDtypeStruct((STEPS,) + latents.shape, F32),
            jax.ShapeDtypeStruct(latents.shape, F32),
        ),
        in_specs=[pl.BlockSpec(memory_space=pltpu.SMEM), vmem, vmem] + [hbm] * 7,
        out_specs=(vmem, vmem),
        scratch_shapes=[pltpu.VMEM(w.shape, w.dtype) for w in weights]
        + [
            pltpu.VMEM((channels, 192), BF16),
            pltpu.VMEM((3 * channels, channels), BF16),
            pltpu.VMEM((channels, channels), BF16),
            pltpu.VMEM((3 * channels, channels), BF16),
            pltpu.VMEM((channels, channels), BF16),
            pltpu.VMEM((80, channels), BF16),
            pltpu.VMEM((row_len, 8, width), F32),
            pltpu.VMEM((192, pixels), BF16),
            pltpu.VMEM((channels, pixels), BF16),
            pltpu.VMEM((channels, pixels), BF16),
            pltpu.VMEM((HEADS, head_dim + 16, pixels), BF16),
            pltpu.VMEM((HEADS, width, pixels), F32),
            pltpu.VMEM((HEADS, width, pixels), BF16),
            pltpu.VMEM((SPAN, channels, width), F32),
            pltpu.VMEM((row_len, 8, width), F32),
            pltpu.VMEM((STEPS, channels, width), BF16),
            pltpu.VMEM((STEPS, 2 * HALF, channels, width), BF16),
            pltpu.VMEM((STEPS, row_len, 24, width), F32),
            pltpu.VMEM((STEPS, 2, 8, width), F32),
            pltpu.VMEM((STEPS, 24, width), F32),
            pltpu.VMEM((STEPS, 2, 8, width), F32),
            dma((7,)),
            dma((row_len,)),
            dma((row_len,)),
            dma((STEPS, 2 * HALF)),
            dma((STEPS, 2 * HALF)),
            dma((STEPS, row_len)),
            dma((STEPS, row_len)),
            dma((STEPS, 2)),
            dma((STEPS, 2)),
        ],
        compiler_params=pltpu.CompilerParams(
            collective_id=0 if comm else None,
            has_side_effects=True,
            vmem_limit_bytes=40 * 1024 * 1024,
        ),
        name="denoise",
    )(timesteps, latents, fresh_noise, *weights)


def solution(mesh):
    sizes = (mesh.shape["queue"], mesh.shape["row"], True)
    return jax.shard_map(
        functools.partial(on_device, sizes=sizes),
        mesh=mesh,
        in_specs=(
            P("queue", None, "row", None),
            P(None, None, "row", None),
            P("queue", None),
            P(),
            P(),
            P(),
            P(),
            P(),
            P(),
            P(),
        ),
        out_specs=(P(None, "queue", None, "row", None), P("queue", None, "row", None)),
        check_vma=False,
    )
```

```python
import functools
import math

import jax
import jax.numpy as jnp
from jax import lax
from jax.experimental import pallas as pl
from jax.experimental.pallas import tpu as pltpu
from jax.sharding import PartitionSpec as P

HEADS = 5
HALF = 4
STEPS = 2
SPAN = 2 * HALF + 1
F32 = jnp.float32
BF16 = jnp.bfloat16
MESH = pl.DeviceIdType.MESH


def dot(left, right):
    return jnp.dot(left, right, preferred_element_type=F32)


def dot_rows(left, right):
    return lax.dot_general(left, right, (((1,), (1,)), ((), ())), preferred_element_type=F32)


def dot_columns(left, right):
    return lax.dot_general(left, right, (((0,), (0,)), ((), ())), preferred_element_type=F32)


def parts_of(values):
    high = values.astype(BF16)
    return high, (values - high.astype(F32)).astype(BF16)


def plan(level):
    start = 0.008 / 1.008 * math.pi / 2.0
    base = math.cos(start) ** 2
    angle = ((level + 1.0) / 1000.0 + 0.008) / 1.008 * (math.pi / 2.0)
    signal = jnp.cos(angle) ** 2 / base
    remain = jnp.sin(angle - start) * jnp.sin(angle + start) / base
    return (signal, remain)


def shifted(tile, step):
    if step == 1:
        return tile
    width = tile.shape[1]
    lane = lax.broadcasted_iota(jnp.int32, tile.shape, 1)
    if step == 0:
        return jnp.where(lane == 0, 0.0, pltpu.roll(tile, 1, 1))
    return jnp.where(lane == width - 1, 0.0, pltpu.roll(tile, width - 1, 1))


def layer_norm_columns(values):
    centre = values - jnp.mean(values, axis=0, keepdims=True)
    return centre * lax.rsqrt(jnp.mean(centre * centre, axis=0, keepdims=True) + 1e-05)


def kernel(
    sizes,
    steps_ref,
    latents_ref,
    noise_ref,
    conv_in_hbm,
    time_hbm,
    spatial_in_hbm,
    spatial_out_hbm,
    temporal_in_hbm,
    temporal_out_hbm,
    conv_out_hbm,
    denoised_ref,
    queue_ref,
    conv_in_ref,
    time_ref,
    spatial_in_ref,
    spatial_out_ref,
    temporal_in_ref,
    temporal_out_ref,
    conv_out_ref,
    conv_in_t,
    score_w,
    mixed_w,
    temporal_in_t,
    temporal_out_t,
    conv_out_t,
    frame_ref,
    patch_ref,
    scaled_ref,
    score_ref,
    weight_ref,
    tkv_ref,
    rows_ref,
    sent_ref,
    beside_ref,
    parts_ref,
    own_out_ref,
    next_out_ref,
    own_in_ref,
    load_sem,
    rows_send,
    rows_recv,
    beside_send,
    beside_recv,
    next_send,
    next_recv,
    own_send,
    own_recv,
):
    queue_len, row_len, comm = sizes
    channels = time_ref.shape[0]
    head_dim = channels // HEADS
    width = latents_ref.shape[3]
    pixels = row_len * width
    if comm:
        me_q = lax.axis_index("queue")
        me_r = lax.axis_index("row")
    else:
        me_q = 5
        me_r = 3
    core = lax.rem(me_q, 2)
    sibling = me_q + 1 - 2 * core
    last_frame = queue_len - 1

    def row_at(offset):
        return lax.rem(me_r + offset + row_len, row_len)

    def send(source, target, send_sem, recv_sem, device):
        return pltpu.make_async_remote_copy(
            src_ref=source,
            dst_ref=target,
            send_sem=send_sem,
            recv_sem=recv_sem,
            device_id=device,
            device_id_type=MESH,
        )

    loads = [
        pltpu.make_async_copy(source, target, load_sem.at[index])
        for index, (source, target) in enumerate(
            (
                (time_hbm, time_ref),
                (conv_in_hbm, conv_in_ref),
                (spatial_in_hbm, spatial_in_ref),
                (spatial_out_hbm, spatial_out_ref),
                (temporal_in_hbm, temporal_in_ref),
                (temporal_out_hbm, temporal_out_ref),
                (conv_out_hbm, conv_out_ref),
            )
        )
    ]
    for load in loads:
        load.start()

    if comm:
        barrier = pltpu.get_barrier_semaphore()

        def greet(q, r):
            pl.semaphore_signal(barrier, inc=1, device_id=(q, r), device_id_type=MESH)

        @pl.when(me_q < last_frame)
        def _():
            for offset in range(row_len):
                greet(me_q + 1, row_at(offset))

        @pl.when(me_q > 0)
        def _():
            for offset in range(row_len):
                greet(me_q - 1, row_at(offset))

        for offset in range(1, row_len):
            greet(me_q, row_at(offset))
        for distance in (2, 4):

            @pl.when(me_q + distance <= last_frame)
            def _():
                greet(me_q + distance, me_r)

            @pl.when(me_q - distance >= 0)
            def _():
                greet(me_q - distance, me_r)

    latents = latents_ref[0, :, 0, :]
    empty = jnp.zeros_like(latents)
    state = jnp.concatenate([latents, empty], axis=0)
    rows_ref[me_r] = jnp.concatenate([latents, noise_ref[0, :, 0, :]], axis=0)

    level_now = steps_ref[0, 0].astype(F32)
    level_next = steps_ref[0, 1].astype(F32)
    signal_now, rest_now = plan(jnp.full((8, width), level_now, F32))
    signal_next, rest_next = plan(jnp.full((8, width), level_next, F32))
    keep = jnp.sqrt(signal_next) / jnp.sqrt(signal_now)
    push = jnp.sqrt(rest_next) - keep * jnp.sqrt(rest_now)

    half = channels // 2
    column = lax.broadcasted_iota(jnp.int32, (8, channels), 1)
    place = jnp.where(column < half, column, column - half).astype(F32)
    angle = level_now * jnp.exp(place * (-math.log(10000.0) / half))
    embedding = jnp.where(column < half, jnp.cos(angle), jnp.sin(angle)).astype(BF16)
    loads[0].wait()
    projected = dot(embedding, time_ref[...])
    bias = projected[0:1] / (1.0 + jnp.exp(-projected[0:1]))
    bias = bias - jnp.mean(bias, axis=1, keepdims=True)

    loads[1].wait()
    wide = conv_in_ref[...].astype(F32)
    wide = wide - jnp.mean(wide, axis=1, keepdims=True)
    gap = jnp.zeros((4, channels), F32)
    lone = jnp.concatenate([bias, gap[0:3]], axis=0)
    centred = jnp.concatenate(
        [wide[0:12], gap, wide[12:24], lone, wide[24:36], gap], axis=0
    )
    rows = centred.shape[0]
    high, low = parts_of(centred)
    conv_in_t[...] = jnp.concatenate([high, low], axis=0).astype(F32).T.astype(BF16)

    if comm:
        def reaches(space, distance):
            return lax.div(space + queue_len - distance, queue_len)

        greeted = row_len - 1
        for space in (me_q, last_frame - me_q):
            greeted += row_len * reaches(space, 1) + reaches(space, 2) + reaches(space, 4)
        pl.semaphore_wait(barrier, greeted)

    row_copies = []
    if comm:
        for offset in range(1, row_len):
            copy = send(
                rows_ref.at[me_r],
                rows_ref.at[me_r],
                rows_send.at[offset],
                rows_recv.at[offset],
                (me_q, row_at(offset)),
            )
            copy.start()
            row_copies.append(copy)

    loads[2].wait()
    seen = dot(high, spatial_in_ref[...]) + dot(low, spatial_in_ref[...])
    head_of = lax.broadcasted_iota(jnp.int32, (rows, channels), 1) // head_dim

    def by_head(values):
        return jnp.concatenate(
            [jnp.where(head_of == head, values, 0.0) for head in range(HEADS)], axis=0
        )

    query_high, query_low = parts_of(seen[:, :channels])
    key_high, key_low = parts_of(by_head(seen[:, channels : 2 * channels]))
    query_high = jnp.concatenate([query_high] * 3, axis=0)
    query_low = jnp.concatenate([query_low] * 3, axis=0)
    product = (
        dot_rows(key_high, query_high)
        + dot_rows(key_high, query_low)
        + dot_rows(key_low, query_high)
    ) * (1.0 / math.sqrt(head_dim))
    high, low = parts_of(product)
    third = lax.broadcasted_iota(jnp.int32, product.shape, 1) // rows
    score_w[...] = jnp.where(third < 2, high.astype(F32), low.astype(F32)).astype(BF16)
    loads[3].wait()
    turned = spatial_out_ref[...].T
    value_high, value_low = parts_of(by_head(seen[:, 2 * channels :]))
    product = dot_rows(turned, value_high) + dot_rows(turned, value_low)
    high, low = parts_of(product)
    mixed_w[0] = high
    mixed_w[1] = low

    loads[4].wait()
    temporal_in_t[...] = temporal_in_ref[...].T
    loads[5].wait()
    temporal_out_t[...] = temporal_out_ref[...].T
    loads[6].wait()
    turned = conv_out_ref[...].astype(F32)
    pieces = []
    for col_step in range(3):
        for row_step in range(3):
            base = 4 * (3 * row_step + col_step)
            pieces.append(turned[base : base + 4])
            pieces.append(gap)
    pieces.append(jnp.zeros((8, channels), F32))
    conv_out_t[...] = jnp.concatenate(pieces, axis=0).astype(BF16)
    scaled_ref[3 * rows :, :] = jnp.ones((16, pixels), BF16)

    for copy in row_copies:
        copy.wait_recv()

    own_columns = pl.ds(pl.multiple_of(me_r * width, width), width)
    sublane = lax.broadcasted_iota(jnp.int32, (8, width), 0)
    upper = sublane < 4
    constant = jnp.where(sublane == 4, 1.0, 0.0)
    unsent = list(row_copies)
    guarded_unsent = []
    own_copies = []
    middles = []
    images = [jnp.where(upper, rows_ref[y], 0.0) for y in range(row_len)]

    for step in range(STEPS):
        tiles = []
        for y in range(row_len):
            tile = images[y]
            tiles.append(
                jnp.concatenate(
                    [shifted(tile, 0) + pltpu.roll(tile, 4, 0), shifted(tile, 2) + constant],
                    axis=0,
                ).astype(BF16)
            )
        nothing = jnp.zeros_like(tiles[0])
        for y in range(row_len):
            for a in range(3):
                other = y + a - 1
                patch_ref[16 * a : 16 * a + 16, y * width : (y + 1) * width] = (
                    tiles[other] if 0 <= other < row_len else nothing
                )

        chunk = 2 * width
        for lower in range(0, pixels, chunk):
            span = slice(lower, lower + chunk)
            patch = patch_ref[:, span]
            hidden = dot(conv_in_t[...], jnp.concatenate([patch, patch], axis=0))
            factor = lax.rsqrt(jnp.mean(hidden * hidden, axis=0, keepdims=True) + 1e-05)
            high, low = parts_of(patch.astype(F32) * factor)
            scaled_ref[0:rows, span] = high
            scaled_ref[rows : 2 * rows, span] = low
            scaled_ref[2 * rows : 3 * rows, span] = high

        patch = patch_ref[:, own_columns]
        hidden = dot(conv_in_t[...], jnp.concatenate([patch, patch], axis=0))
        queries = dot(score_w[...], scaled_ref[0 : 3 * rows, own_columns])

        mixed = []
        for head in range(HEADS):
            high, low = parts_of(queries[head * rows : (head + 1) * rows])
            score_ref[head] = dot_columns(
                jnp.concatenate([high, high, low], axis=0), scaled_ref[0 : 3 * rows, :]
            )
            for lower in range(0, width, 32):
                block = score_ref[head, lower : lower + 32, :]
                peak = jnp.max(block, axis=1, keepdims=True)
                weight_ref[head, lower : lower + 32, :] = jnp.exp(block - peak).astype(BF16)
            summed = dot_rows(scaled_ref[rows:, :], weight_ref[head])
            mixed.append(
                (summed[0:rows] + summed[rows : 2 * rows]) / summed[2 * rows : 2 * rows + 1]
            )
        high, low = parts_of(jnp.concatenate(mixed, axis=0))
        hidden = hidden + dot(mixed_w[0], high) + dot(mixed_w[0], low) + dot(mixed_w[1], high)
        normed = layer_norm_columns(hidden).astype(BF16)
        sent_ref[step] = normed

        within = (
            me_q >= 2,
            me_q + 2 <= last_frame,
            me_q >= 4,
            me_q + 4 <= last_frame,
        )
        if comm:
            direct = []
            for slot, offset in enumerate((2, -2, 4, -4)):
                copy = send(
                    sent_ref.at[step],
                    beside_ref.at[step, slot],
                    beside_send.at[step, slot],
                    beside_recv.at[step, slot],
                    (me_q + offset, me_r),
                )
                direct.append(copy)
                target = me_q + offset
                reachable = jnp.logical_and(target >= 0, target <= last_frame)
                pl.when(reachable)(copy.start)
                guarded_unsent.append((reachable, copy))
            near = send(
                sent_ref.at[step],
                beside_ref.at[step, 4],
                beside_send.at[step, 4],
                beside_recv.at[step, 4],
                (sibling, me_r),
            )
            near.start()
            unsent.append(near)

        projected = dot(temporal_in_t[...], normed).astype(BF16).astype(F32)
        tqueries = projected[:channels] * (1.0 / math.sqrt(head_dim))
        tkv_ref[2 * HALF] = projected[2 * channels :]
        scores = [None] * SPAN

        def score_of(keys):
            return jnp.concatenate(
                [
                    jnp.sum(
                        tqueries[h * head_dim : (h + 1) * head_dim]
                        * keys[h * head_dim : (h + 1) * head_dim],
                        axis=0,
                        keepdims=True,
                    )
                    for h in range(HEADS)
                ],
                axis=0,
            )

        def take(slots):
            joined = [beside_ref[step, slot] for slot in slots]
            joined = joined[0] if len(slots) == 1 else jnp.concatenate(joined, axis=1)
            projected = dot(temporal_in_t[channels:, :], joined).astype(BF16).astype(F32)
            for inner, slot in enumerate(slots):
                part = projected[:, inner * width : (inner + 1) * width]
                scores[slot] = score_of(part[:channels])
                tkv_ref[slot] = part[channels:]

        scores[2 * HALF] = score_of(projected[channels : 2 * channels])
        far = 3 - core
        outer = 2 + core
        far_within = jnp.where(core == 0, me_q + 4, queue_len + 3 - me_q) <= last_frame
        outer_within = jnp.where(core == 0, me_q, last_frame - me_q) >= 4
        if comm:
            near.wait_recv()
        take([4])
        if comm:

            def received(slot, good):
                copy = send(
                    sent_ref.at[step],
                    beside_ref.at[step, slot],
                    beside_send.at[step, slot],
                    beside_recv.at[step, slot],
                    (sibling, me_r),
                )
                pl.when(good)(copy.wait_recv)

                @pl.when(jnp.logical_not(good))
                def _():
                    beside_ref[step, slot] = jnp.zeros((channels, width), BF16)

            def forward(slot, target, good):
                received(slot, good)
                copy = send(
                    beside_ref.at[step, slot],
                    beside_ref.at[step, target],
                    beside_send.at[step, target],
                    beside_recv.at[step, target],
                    (sibling, me_r),
                )
                copy.start()
                unsent.append(copy)
                return copy

            third = forward(far, 7, far_within)
            first = forward(0, 5, within[0])
            second = forward(1, 6, within[1])
            received(outer, outer_within)
        take([0, 1])
        take([2, 3])
        if comm:
            first.wait_recv()
            third.wait_recv()
        take([5, 7])
        if comm:
            second.wait_recv()
        take([6])

        away = sibling - me_q
        frames = (
            me_q - 2,
            me_q + 2,
            me_q - 4,
            me_q + 4,
            sibling,
            sibling - 2,
            sibling + 2,
            me_q - 3 * away,
        )
        for slot, frame in enumerate(frames):
            good = jnp.logical_and(frame >= 0, frame <= last_frame)
            scores[slot] = jnp.where(good, scores[slot], -jnp.inf)
        peak = functools.reduce(jnp.maximum, scores)
        weights = [jnp.exp(score - peak) for score in scores]
        total = functools.reduce(jnp.add, weights)
        rounded = [weight.astype(BF16).astype(F32) for weight in weights]
        mixed = []
        for head in range(HEADS):
            blended = None
            for index in range(SPAN):
                term = (
                    rounded[index][head : head + 1]
                    * tkv_ref[index, head * head_dim : (head + 1) * head_dim, :]
                )
                blended = term if blended is None else blended + term
            mixed.append(blended / total[head : head + 1])
        mixed = jnp.concatenate(mixed, axis=0).astype(BF16)
        hidden = hidden + dot(temporal_out_t[...], mixed)
        normed = layer_norm_columns(hidden).astype(BF16)

        taps = dot(conv_out_t[...], normed)
        added = shifted(taps[0:24], 0) + taps[24:48] + shifted(taps[48:72], 2)
        below = push * added[0:8]
        middle = push * added[8:16] + keep * state
        above = push * added[16:24]
        middles.append(middle)
        own_out_ref[step, 0] = below
        own_out_ref[step, 1] = above
        next_out_ref[step, 0:8] = middle
        next_out_ref[step, 8:16] = below + pltpu.roll(above, 4, 0)

        last = step == STEPS - 1
        next_copies = []
        if comm:
            for offset in (0, 1, row_len - 1) if last else range(row_len):
                copy = send(
                    next_out_ref.at[step],
                    parts_ref.at[step, me_r],
                    next_send.at[step, offset],
                    next_recv.at[step, offset],
                    (me_q - 1, row_at(offset)),
                )
                pl.when(me_q > 0)(copy.start)
                guarded_unsent.append((me_q > 0, copy))
                next_copies.append(copy)
            for slot, offset in enumerate((1, -1)):
                copy = send(
                    own_out_ref.at[step, slot],
                    own_in_ref.at[step, slot],
                    own_send.at[step, slot],
                    own_recv.at[step, slot],
                    (me_q, row_at(offset)),
                )
                copy.start()
                own_copies.append(copy)
            for copy in next_copies:
                pl.when(me_q < last_frame)(copy.wait_recv)
        entering = me_q == last_frame
        if not last:
            images = []
            for y in range(row_len):
                total = parts_ref[step, y, 0:8]
                if y > 0:
                    total = total + parts_ref[step, y - 1, 8:16]
                if y < row_len - 1:
                    total = total + pltpu.roll(parts_ref[step, y + 1, 8:16], 4, 0)
                total = jnp.where(entering, pltpu.roll(rows_ref[y], 4, 0), total)
                total = jnp.where(upper, total, 0.0)
                images.append(total)
                frame_ref[y] = total
            state = frame_ref[me_r]
        else:
            total = parts_ref[step, me_r, 0:8]
            total = total + jnp.where(me_r == 0, 0.0, parts_ref[step, row_at(-1), 8:16])
            total = total + jnp.where(
                me_r == row_len - 1, 0.0, pltpu.roll(parts_ref[step, row_at(1), 8:16], 4, 0)
            )
            queue_ref[0, :, 0, :] = jnp.where(entering, noise_ref[step, :, 0, :], total[0:4])

    for copy in own_copies:
        copy.wait()
    for step in range(STEPS):
        total = middles[step]
        total = total + jnp.where(me_r == 0, 0.0, own_in_ref[step, 0])
        total = total + jnp.where(me_r == row_len - 1, 0.0, own_in_ref[step, 1])
        denoised_ref[step, 0, :, 0, :] = total[0:4]
    for copy in unsent:
        copy.wait_send()
    for reachable, copy in guarded_unsent:
        pl.when(reachable)(copy.wait_send)


def on_device(
    latents,
    fresh_noise,
    timesteps,
    conv_in_w,
    time_w,
    spatial_in,
    spatial_out,
    temporal_in,
    temporal_out,
    conv_out_w,
    *,
    sizes,
):
    queue_len, row_len, comm = sizes
    channels = conv_in_w.shape[1]
    width = latents.shape[3]
    pixels = row_len * width
    vmem = pl.BlockSpec(memory_space=pltpu.VMEM)
    hbm = pl.BlockSpec(memory_space=pl.ANY)
    dma = pltpu.SemaphoreType.DMA
    weights = (conv_in_w, time_w, spatial_in, spatial_out, temporal_in, temporal_out, conv_out_w.T)
    return pl.pallas_call(
        functools.partial(kernel, sizes),
        out_shape=(
            jax.ShapeDtypeStruct((STEPS,) + latents.shape, F32),
            jax.ShapeDtypeStruct(latents.shape, F32),
        ),
        in_specs=[pl.BlockSpec(memory_space=pltpu.SMEM), vmem, vmem] + [hbm] * 7,
        out_specs=(vmem, vmem),
        scratch_shapes=[pltpu.VMEM(w.shape, w.dtype) for w in weights]
        + [
            pltpu.VMEM((channels, 96), BF16),
            pltpu.VMEM((HEADS * 48, 144), BF16),
            pltpu.VMEM((2, channels, HEADS * 48), BF16),
            pltpu.VMEM((3 * channels, channels), BF16),
            pltpu.VMEM((channels, channels), BF16),
            pltpu.VMEM((80, channels), BF16),
            pltpu.VMEM((row_len, 8, width), F32),
            pltpu.VMEM((48, pixels), BF16),
            pltpu.VMEM((160, pixels), BF16),
            pltpu.VMEM((HEADS, width, pixels), F32),
            pltpu.VMEM((HEADS, width, pixels), BF16),
            pltpu.VMEM((SPAN, channels, width), F32),
            pltpu.VMEM((row_len, 8, width), F32),
            pltpu.VMEM((STEPS, channels, width), BF16),
            pltpu.VMEM((STEPS, 2 * HALF, channels, width), BF16),
            pltpu.VMEM((STEPS, row_len, 16, width), F32),
            pltpu.VMEM((STEPS, 2, 8, width), F32),
            pltpu.VMEM((STEPS, 16, width), F32),
            pltpu.VMEM((STEPS, 2, 8, width), F32),
            dma((7,)),
            dma((row_len,)),
            dma((row_len,)),
            dma((STEPS, 2 * HALF)),
            dma((STEPS, 2 * HALF)),
            dma((STEPS, row_len)),
            dma((STEPS, row_len)),
            dma((STEPS, 2)),
            dma((STEPS, 2)),
        ],
        compiler_params=pltpu.CompilerParams(
            collective_id=0 if comm else None,
            has_side_effects=True,
            vmem_limit_bytes=60 * 1024 * 1024,
        ),
        name="denoise",
    )(timesteps, latents, fresh_noise, *weights)


def solution(mesh):
    sizes = (mesh.shape["queue"], mesh.shape["row"], True)
    return jax.shard_map(
        functools.partial(on_device, sizes=sizes),
        mesh=mesh,
        in_specs=(
            P("queue", None, "row", None),
            P(None, None, "row", None),
            P("queue", None),
            P(),
            P(),
            P(),
            P(),
            P(),
            P(),
            P(),
        ),
        out_specs=(P(None, "queue", None, "row", None), P("queue", None, "row", None)),
        check_vma=False,
    )
```

```python
import functools
import math

import jax
import jax.numpy as jnp
from jax import lax
from jax.experimental import pallas as pl
from jax.experimental.pallas import tpu as pltpu
from jax.sharding import PartitionSpec as P

HEADS = 5
HALF = 4
STEPS = 2
SPAN = 2 * HALF + 1
F32 = jnp.float32
BF16 = jnp.bfloat16
MESH = pl.DeviceIdType.MESH


def dot(left, right):
    return jnp.dot(left, right, preferred_element_type=F32)


def dot_rows(left, right):
    return lax.dot_general(left, right, (((1,), (1,)), ((), ())), preferred_element_type=F32)


def dot_columns(left, right):
    return lax.dot_general(left, right, (((0,), (0,)), ((), ())), preferred_element_type=F32)


def parts_of(values):
    high = values.astype(BF16)
    return high, (values - high.astype(F32)).astype(BF16)


def plan(level):
    start = 0.008 / 1.008 * math.pi / 2.0
    base = math.cos(start) ** 2
    angle = ((level + 1.0) / 1000.0 + 0.008) / 1.008 * (math.pi / 2.0)
    signal = jnp.cos(angle) ** 2 / base
    remain = jnp.sin(angle - start) * jnp.sin(angle + start) / base
    return (signal, remain)


def shifted(tile, step):
    if step == 1:
        return tile
    width = tile.shape[1]
    lane = lax.broadcasted_iota(jnp.int32, tile.shape, 1)
    if step == 0:
        return jnp.where(lane == 0, 0.0, pltpu.roll(tile, 1, 1))
    return jnp.where(lane == width - 1, 0.0, pltpu.roll(tile, width - 1, 1))


def layer_norm_columns(values):
    centre = values - jnp.mean(values, axis=0, keepdims=True)
    return centre * lax.rsqrt(jnp.mean(centre * centre, axis=0, keepdims=True) + 1e-05)


def kernel(
    sizes,
    steps_ref,
    latents_ref,
    noise_ref,
    conv_in_hbm,
    time_hbm,
    spatial_in_hbm,
    spatial_out_hbm,
    temporal_in_hbm,
    temporal_out_hbm,
    conv_out_hbm,
    denoised_ref,
    queue_ref,
    conv_in_ref,
    time_ref,
    spatial_in_ref,
    spatial_out_ref,
    temporal_in_ref,
    temporal_out_ref,
    conv_out_ref,
    conv_in_t,
    score_w,
    mixed_w,
    temporal_in_t,
    temporal_out_t,
    conv_out_t,
    frame_ref,
    entered_ref,
    patch_ref,
    scaled_ref,
    score_ref,
    weight_ref,
    tkv_ref,
    rows_ref,
    sent_ref,
    beside_ref,
    parts_ref,
    own_out_ref,
    next_out_ref,
    own_in_ref,
    load_sem,
    rows_send,
    rows_recv,
    beside_send,
    beside_recv,
    next_send,
    next_recv,
    own_send,
    own_recv,
):
    queue_len, row_len, comm = sizes
    channels = time_ref.shape[0]
    head_dim = channels // HEADS
    width = latents_ref.shape[3]
    pixels = row_len * width
    if comm:
        me_q = lax.axis_index("queue")
        me_r = lax.axis_index("row")
    else:
        me_q = 5
        me_r = 3
    core = lax.rem(me_q, 2)
    sibling = me_q + 1 - 2 * core
    last_frame = queue_len - 1

    def row_at(offset):
        return lax.rem(me_r + offset + row_len, row_len)

    def send(source, target, send_sem, recv_sem, device):
        return pltpu.make_async_remote_copy(
            src_ref=source,
            dst_ref=target,
            send_sem=send_sem,
            recv_sem=recv_sem,
            device_id=device,
            device_id_type=MESH,
        )

    loads = [
        pltpu.make_async_copy(source, target, load_sem.at[index])
        for index, (source, target) in enumerate(
            (
                (time_hbm, time_ref),
                (conv_in_hbm, conv_in_ref),
                (spatial_in_hbm, spatial_in_ref),
                (spatial_out_hbm, spatial_out_ref),
                (temporal_in_hbm, temporal_in_ref),
                (temporal_out_hbm, temporal_out_ref),
                (conv_out_hbm, conv_out_ref),
            )
        )
    ]
    for load in loads:
        load.start()

    if comm:
        barrier = pltpu.get_barrier_semaphore()

        def greet(q, r):
            pl.semaphore_signal(barrier, inc=1, device_id=(q, r), device_id_type=MESH)

        for offset in range(1, row_len):
            greet(me_q, row_at(offset))
        greet(sibling, me_r)
        for distance in (2, 4):

            @pl.when(me_q + distance <= last_frame)
            def _():
                greet(me_q + distance, me_r)

            @pl.when(me_q - distance >= 0)
            def _():
                greet(me_q - distance, me_r)

    latents = latents_ref[0, :, 0, :]
    empty = jnp.zeros_like(latents)
    state = jnp.concatenate([latents, empty], axis=0)
    rows_ref[me_r] = jnp.concatenate([latents, noise_ref[0, :, 0, :]], axis=0)

    level_now = steps_ref[0, 0].astype(F32)
    level_next = steps_ref[0, 1].astype(F32)
    signal_now, rest_now = plan(jnp.full((8, width), level_now, F32))
    signal_next, rest_next = plan(jnp.full((8, width), level_next, F32))
    keep = jnp.sqrt(signal_next) / jnp.sqrt(signal_now)
    push = jnp.sqrt(rest_next) - keep * jnp.sqrt(rest_now)

    half = channels // 2
    column = lax.broadcasted_iota(jnp.int32, (8, channels), 1)
    place = jnp.where(column < half, column, column - half).astype(F32)
    angle = level_now * jnp.exp(place * (-math.log(10000.0) / half))
    embedding = jnp.where(column < half, jnp.cos(angle), jnp.sin(angle)).astype(BF16)
    loads[0].wait()
    projected = dot(embedding, time_ref[...])
    bias = projected[0:1] / (1.0 + jnp.exp(-projected[0:1]))
    bias = bias - jnp.mean(bias, axis=1, keepdims=True)

    loads[1].wait()
    wide = conv_in_ref[...].astype(F32)
    wide = wide - jnp.mean(wide, axis=1, keepdims=True)
    gap = jnp.zeros((4, channels), F32)
    lone = jnp.concatenate([bias, gap[0:3]], axis=0)
    centred = jnp.concatenate(
        [wide[0:12], gap, wide[12:24], lone, wide[24:36], gap], axis=0
    )
    rows = centred.shape[0]
    high, low = parts_of(centred)
    conv_in_t[...] = jnp.concatenate([high, low], axis=0).astype(F32).T.astype(BF16)

    if comm:
        def reaches(space, distance):
            return lax.div(space + queue_len - distance, queue_len)

        greeted = row_len
        for space in (me_q, last_frame - me_q):
            greeted += reaches(space, 2) + reaches(space, 4)
        pl.semaphore_wait(barrier, greeted)

    row_copies = []
    if comm:
        for offset in range(1, row_len):
            copy = send(
                rows_ref.at[me_r],
                rows_ref.at[me_r],
                rows_send.at[offset],
                rows_recv.at[offset],
                (me_q, row_at(offset)),
            )
            copy.start()
            row_copies.append(copy)

    loads[2].wait()
    seen = dot(high, spatial_in_ref[...]) + dot(low, spatial_in_ref[...])
    head_of = lax.broadcasted_iota(jnp.int32, (rows, channels), 1) // head_dim

    def by_head(values, slots=False):
        pieces = []
        for head in range(HEADS):
            own = jnp.where(head_of == head, values, 0.0)
            pieces += [own, own, jnp.zeros((128 - 2 * rows, channels), F32)] if slots else [own]
        return jnp.concatenate(pieces, axis=0)

    query_high, query_low = parts_of(seen[:, :channels])
    key_high, key_low = parts_of(by_head(seen[:, channels : 2 * channels], True))
    product = (
        dot_rows(query_high, key_high)
        + dot_rows(query_low, key_high)
        + dot_rows(query_high, key_low)
    ) * (1.0 / math.sqrt(head_dim))
    high, low = parts_of(product)
    score_w[0:rows] = high
    score_w[rows : 2 * rows] = high
    score_w[2 * rows : 128] = jnp.zeros((128 - 2 * rows, HEADS * 128), BF16)
    score_w[128 : 128 + rows] = low
    loads[3].wait()
    turned = spatial_out_ref[...].T
    value_high, value_low = parts_of(by_head(seen[:, 2 * channels :]))
    product = dot_rows(turned, value_high) + dot_rows(turned, value_low)
    high, low = parts_of(product)
    mixed_w[0] = high
    mixed_w[1] = low

    loads[4].wait()
    temporal_in_t[...] = temporal_in_ref[...].T
    loads[5].wait()
    temporal_out_t[...] = temporal_out_ref[...].T
    loads[6].wait()
    turned = conv_out_ref[...].astype(F32)
    pieces = []
    for col_step in range(3):
        for row_step in range(3):
            base = 4 * (3 * row_step + col_step)
            pieces.append(turned[base : base + 4])
            pieces.append(gap)
    pieces.append(jnp.zeros((8, channels), F32))
    conv_out_t[...] = jnp.concatenate(pieces, axis=0).astype(BF16)
    scaled_ref[2 * rows : 2 * rows + 16, :] = jnp.ones((16, pixels), BF16)
    scaled_ref[2 * rows + 16 : 128, :] = jnp.zeros((128 - 2 * rows - 16, pixels), BF16)
    scaled_ref[128 + rows :, :] = jnp.zeros((128 - rows, pixels), BF16)

    for copy in row_copies:
        copy.wait_recv()

    own_columns = pl.ds(pl.multiple_of(me_r * width, width), width)
    sublane = lax.broadcasted_iota(jnp.int32, (8, width), 0)
    upper = sublane < 4
    constant = jnp.where(sublane == 4, 1.0, 0.0)
    unsent = list(row_copies)
    guarded_unsent = []
    own_copies = []
    middles = []
    images = []
    for y in range(row_len):
        images.append(jnp.where(upper, rows_ref[y], 0.0))
        entered_ref[y] = jnp.where(upper, pltpu.roll(rows_ref[y], 4, 0), 0.0)

    for step in range(STEPS):
        tiles = []
        for y in range(row_len):
            tile = images[y]
            tiles.append(
                jnp.concatenate(
                    [shifted(tile, 0) + pltpu.roll(tile, 4, 0), shifted(tile, 2) + constant],
                    axis=0,
                ).astype(BF16)
            )
        nothing = jnp.zeros_like(tiles[0])
        for y in range(row_len):
            for a in range(3):
                other = y + a - 1
                patch_ref[16 * a : 16 * a + 16, y * width : (y + 1) * width] = (
                    tiles[other] if 0 <= other < row_len else nothing
                )

        chunk = 2 * width
        for lower in range(0, pixels, chunk):
            span = slice(lower, lower + chunk)
            patch = patch_ref[:, span]
            hidden = dot(conv_in_t[...], jnp.concatenate([patch, patch], axis=0))
            factor = lax.rsqrt(jnp.mean(hidden * hidden, axis=0, keepdims=True) + 1e-05)
            high, low = parts_of(patch.astype(F32) * factor)
            scaled_ref[0:rows, span] = high
            scaled_ref[rows : 2 * rows, span] = low
            scaled_ref[128 : 128 + rows, span] = high

        patch = patch_ref[:, own_columns]
        hidden = dot(conv_in_t[...], jnp.concatenate([patch, patch], axis=0))
        queries = dot_columns(scaled_ref[0 : 128 + rows, own_columns], score_w[...])
        high, low = parts_of(queries)
        lefts = [
            jnp.concatenate(
                [high[:, 128 * head : 128 * head + 128], low[:, 128 * head : 128 * head + 128]],
                axis=1,
            )
            for head in range(HEADS)
        ]
        score_ref[...] = dot(jnp.concatenate(lefts, axis=0), scaled_ref[...])
        for lower in range(0, HEADS * width, 32):
            block = score_ref[lower : lower + 32, :]
            peak = jnp.max(block, axis=1, keepdims=True)
            weight_ref[lower : lower + 32, :] = jnp.exp(block - peak).astype(BF16)
        summed = dot_rows(scaled_ref[rows : 128 + rows, :], weight_ref[...])
        mixed = (summed[0:rows] + summed[128 - rows : 128]) / summed[rows : rows + 1]
        high, low = parts_of(
            jnp.concatenate(
                [mixed[:, width * head : width * (head + 1)] for head in range(HEADS)], axis=0
            )
        )
        hidden = hidden + dot(mixed_w[0], high) + dot(mixed_w[0], low) + dot(mixed_w[1], high)
        normed = layer_norm_columns(hidden).astype(BF16)
        sent_ref[step] = normed

        within = (
            me_q >= 2,
            me_q + 2 <= last_frame,
            me_q >= 4,
            me_q + 4 <= last_frame,
        )
        if comm:
            direct = []
            for slot, offset in enumerate((2, -2, 4, -4)):
                copy = send(
                    sent_ref.at[step],
                    beside_ref.at[step, slot],
                    beside_send.at[step, slot],
                    beside_recv.at[step, slot],
                    (me_q + offset, me_r),
                )
                direct.append(copy)
                target = me_q + offset
                reachable = jnp.logical_and(target >= 0, target <= last_frame)
                pl.when(reachable)(copy.start)
                guarded_unsent.append((reachable, copy))
            near = send(
                sent_ref.at[step],
                beside_ref.at[step, 4],
                beside_send.at[step, 4],
                beside_recv.at[step, 4],
                (sibling, me_r),
            )
            near.start()
            unsent.append(near)

        projected = dot(temporal_in_t[...], normed).astype(BF16).astype(F32)
        tqueries = projected[:channels] * (1.0 / math.sqrt(head_dim))
        tkv_ref[2 * HALF] = projected[2 * channels :]
        scores = [None] * SPAN

        def score_of(keys):
            return jnp.concatenate(
                [
                    jnp.sum(
                        tqueries[h * head_dim : (h + 1) * head_dim]
                        * keys[h * head_dim : (h + 1) * head_dim],
                        axis=0,
                        keepdims=True,
                    )
                    for h in range(HEADS)
                ],
                axis=0,
            )

        def take(slots):
            joined = [beside_ref[step, slot] for slot in slots]
            joined = joined[0] if len(slots) == 1 else jnp.concatenate(joined, axis=1)
            projected = dot(temporal_in_t[channels:, :], joined).astype(BF16).astype(F32)
            for inner, slot in enumerate(slots):
                part = projected[:, inner * width : (inner + 1) * width]
                scores[slot] = score_of(part[:channels])
                tkv_ref[slot] = part[channels:]

        scores[2 * HALF] = score_of(projected[channels : 2 * channels])
        far = 3 - core
        outer = 2 + core
        far_within = jnp.where(core == 0, me_q + 4, queue_len + 3 - me_q) <= last_frame
        outer_within = jnp.where(core == 0, me_q, last_frame - me_q) >= 4
        if comm:
            near.wait_recv()
        take([4])
        if comm:

            def received(slot, good):
                copy = send(
                    sent_ref.at[step],
                    beside_ref.at[step, slot],
                    beside_send.at[step, slot],
                    beside_recv.at[step, slot],
                    (sibling, me_r),
                )
                pl.when(good)(copy.wait_recv)

                @pl.when(jnp.logical_not(good))
                def _():
                    beside_ref[step, slot] = jnp.zeros((channels, width), BF16)

            def forward(slot, target, good):
                received(slot, good)
                copy = send(
                    beside_ref.at[step, slot],
                    beside_ref.at[step, target],
                    beside_send.at[step, target],
                    beside_recv.at[step, target],
                    (sibling, me_r),
                )
                copy.start()
                unsent.append(copy)
                return copy

            third = forward(far, 7, far_within)
            received(outer, outer_within)
        take([2, 3])
        if comm:
            first = forward(0, 5, within[0])
            second = forward(1, 6, within[1])
        take([0, 1])
        if comm:
            first.wait_recv()
            third.wait_recv()
        take([5, 7])
        if comm:
            second.wait_recv()
        take([6])

        away = sibling - me_q
        frames = (
            me_q - 2,
            me_q + 2,
            me_q - 4,
            me_q + 4,
            sibling,
            sibling - 2,
            sibling + 2,
            me_q - 3 * away,
        )
        for slot, frame in enumerate(frames):
            good = jnp.logical_and(frame >= 0, frame <= last_frame)
            scores[slot] = jnp.where(good, scores[slot], -jnp.inf)
        peak = functools.reduce(jnp.maximum, scores)
        weights = [jnp.exp(score - peak) for score in scores]
        total = functools.reduce(jnp.add, weights)
        rounded = [weight.astype(BF16).astype(F32) for weight in weights]
        mixed = []
        for head in range(HEADS):
            blended = None
            for index in range(SPAN):
                term = (
                    rounded[index][head : head + 1]
                    * tkv_ref[index, head * head_dim : (head + 1) * head_dim, :]
                )
                blended = term if blended is None else blended + term
            mixed.append(blended / total[head : head + 1])
        mixed = jnp.concatenate(mixed, axis=0).astype(BF16)
        hidden = hidden + dot(temporal_out_t[...], mixed)
        normed = layer_norm_columns(hidden).astype(BF16)

        taps = dot(conv_out_t[...], normed)
        added = shifted(taps[0:24], 0) + taps[24:48] + shifted(taps[48:72], 2)
        below = push * added[0:8]
        middle = push * added[8:16] + keep * state
        above = push * added[16:24]
        middles.append(middle)
        own_out_ref[step, 0] = below
        own_out_ref[step, 1] = above
        next_out_ref[step, 0:8] = middle
        next_out_ref[step, 8:16] = below + pltpu.roll(above, 4, 0)

        last = step == STEPS - 1
        next_copies = []
        if comm:
            for offset in (0, 1, row_len - 1) if last else range(row_len):
                copy = send(
                    next_out_ref.at[step],
                    parts_ref.at[step, me_r],
                    next_send.at[step, offset],
                    next_recv.at[step, offset],
                    (me_q - 1, row_at(offset)),
                )
                pl.when(me_q > 0)(copy.start)
                guarded_unsent.append((me_q > 0, copy))
                next_copies.append(copy)
            for slot, offset in enumerate((1, -1)):
                copy = send(
                    own_out_ref.at[step, slot],
                    own_in_ref.at[step, slot],
                    own_send.at[step, slot],
                    own_recv.at[step, slot],
                    (me_q, row_at(offset)),
                )
                copy.start()
                own_copies.append(copy)
            for copy in next_copies:
                pl.when(me_q < last_frame)(copy.wait_recv)
        entering = me_q == last_frame
        if not last:
            images = []
            for y in range(row_len):
                total = parts_ref[step, y, 0:8]
                if y > 0:
                    total = total + parts_ref[step, y - 1, 8:16]
                if y < row_len - 1:
                    total = total + pltpu.roll(parts_ref[step, y + 1, 8:16], 4, 0)
                total = jnp.where(entering, entered_ref[y], jnp.where(upper, total, 0.0))
                images.append(total)
                frame_ref[y] = total
            state = frame_ref[me_r]
        else:
            total = parts_ref[step, me_r, 0:8]
            total = total + jnp.where(me_r == 0, 0.0, parts_ref[step, row_at(-1), 8:16])
            total = total + jnp.where(
                me_r == row_len - 1, 0.0, pltpu.roll(parts_ref[step, row_at(1), 8:16], 4, 0)
            )
            queue_ref[0, :, 0, :] = jnp.where(entering, noise_ref[step, :, 0, :], total[0:4])

    for copy in own_copies:
        copy.wait()
    for step in range(STEPS):
        total = middles[step]
        total = total + jnp.where(me_r == 0, 0.0, own_in_ref[step, 0])
        total = total + jnp.where(me_r == row_len - 1, 0.0, own_in_ref[step, 1])
        denoised_ref[step, 0, :, 0, :] = total[0:4]
    for copy in unsent:
        copy.wait_send()
    for reachable, copy in guarded_unsent:
        pl.when(reachable)(copy.wait_send)


def on_device(
    latents,
    fresh_noise,
    timesteps,
    conv_in_w,
    time_w,
    spatial_in,
    spatial_out,
    temporal_in,
    temporal_out,
    conv_out_w,
    *,
    sizes,
):
    queue_len, row_len, comm = sizes
    channels = conv_in_w.shape[1]
    width = latents.shape[3]
    pixels = row_len * width
    vmem = pl.BlockSpec(memory_space=pltpu.VMEM)
    hbm = pl.BlockSpec(memory_space=pl.ANY)
    dma = pltpu.SemaphoreType.DMA
    weights = (conv_in_w, time_w, spatial_in, spatial_out, temporal_in, temporal_out, conv_out_w.T)
    return pl.pallas_call(
        functools.partial(kernel, sizes),
        out_shape=(
            jax.ShapeDtypeStruct((STEPS,) + latents.shape, F32),
            jax.ShapeDtypeStruct(latents.shape, F32),
        ),
        in_specs=[pl.BlockSpec(memory_space=pltpu.SMEM), vmem, vmem] + [hbm] * 7,
        out_specs=(vmem, vmem),
        scratch_shapes=[pltpu.VMEM(w.shape, w.dtype) for w in weights]
        + [
            pltpu.VMEM((channels, 96), BF16),
            pltpu.VMEM((176, HEADS * 128), BF16),
            pltpu.VMEM((2, channels, HEADS * 48), BF16),
            pltpu.VMEM((3 * channels, channels), BF16),
            pltpu.VMEM((channels, channels), BF16),
            pltpu.VMEM((80, channels), BF16),
            pltpu.VMEM((row_len, 8, width), F32),
            pltpu.VMEM((row_len, 8, width), F32),
            pltpu.VMEM((48, pixels), BF16),
            pltpu.VMEM((256, pixels), BF16),
            pltpu.VMEM((HEADS * width, pixels), F32),
            pltpu.VMEM((HEADS * width, pixels), BF16),
            pltpu.VMEM((SPAN, channels, width), F32),
            pltpu.VMEM((row_len, 8, width), F32),
            pltpu.VMEM((STEPS, channels, width), BF16),
            pltpu.VMEM((STEPS, 2 * HALF, channels, width), BF16),
            pltpu.VMEM((STEPS, row_len, 16, width), F32),
            pltpu.VMEM((STEPS, 2, 8, width), F32),
            pltpu.VMEM((STEPS, 16, width), F32),
            pltpu.VMEM((STEPS, 2, 8, width), F32),
            dma((7,)),
            dma((row_len,)),
            dma((row_len,)),
            dma((STEPS, 2 * HALF)),
            dma((STEPS, 2 * HALF)),
            dma((STEPS, row_len)),
            dma((STEPS, row_len)),
            dma((STEPS, 2)),
            dma((STEPS, 2)),
        ],
        compiler_params=pltpu.CompilerParams(
            collective_id=0 if comm else None,
            has_side_effects=True,
            vmem_limit_bytes=60 * 1024 * 1024,
        ),
        name="denoise",
    )(timesteps, latents, fresh_noise, *weights)


def solution(mesh):
    sizes = (mesh.shape["queue"], mesh.shape["row"], True)
    return jax.shard_map(
        functools.partial(on_device, sizes=sizes),
        mesh=mesh,
        in_specs=(
            P("queue", None, "row", None),
            P(None, None, "row", None),
            P("queue", None),
            P(),
            P(),
            P(),
            P(),
            P(),
            P(),
            P(),
        ),
        out_specs=(P(None, "queue", None, "row", None), P("queue", None, "row", None)),
        check_vma=False,
    )
```

```python
import functools
import math

import jax
import jax.numpy as jnp
from jax import lax
from jax.experimental import pallas as pl
from jax.experimental.pallas import tpu as pltpu
from jax.sharding import PartitionSpec as P

HEADS = 5
HALF = 4
STEPS = 2
SPAN = 2 * HALF + 1
F32 = jnp.float32
BF16 = jnp.bfloat16
MESH = pl.DeviceIdType.MESH


def dot(left, right):
    return jnp.dot(left, right, preferred_element_type=F32)


def dot_rows(left, right):
    return lax.dot_general(left, right, (((1,), (1,)), ((), ())), preferred_element_type=F32)


def dot_columns(left, right):
    return lax.dot_general(left, right, (((0,), (0,)), ((), ())), preferred_element_type=F32)


def parts_of(values):
    high = values.astype(BF16)
    return high, (values - high.astype(F32)).astype(BF16)


def plan(level):
    start = 0.008 / 1.008 * math.pi / 2.0
    base = math.cos(start) ** 2
    angle = ((level + 1.0) / 1000.0 + 0.008) / 1.008 * (math.pi / 2.0)
    signal = jnp.cos(angle) ** 2 / base
    remain = jnp.sin(angle - start) * jnp.sin(angle + start) / base
    return (signal, remain)


def shifted(tile, step):
    if step == 1:
        return tile
    width = tile.shape[1]
    lane = lax.broadcasted_iota(jnp.int32, tile.shape, 1)
    if step == 0:
        return jnp.where(lane == 0, 0.0, pltpu.roll(tile, 1, 1))
    return jnp.where(lane == width - 1, 0.0, pltpu.roll(tile, width - 1, 1))


def layer_norm_columns(values):
    centre = values - jnp.mean(values, axis=0, keepdims=True)
    return centre * lax.rsqrt(jnp.mean(centre * centre, axis=0, keepdims=True) + 1e-05)


def kernel(
    sizes,
    steps_hbm,
    latents_hbm,
    noise_hbm,
    conv_in_hbm,
    time_hbm,
    spatial_in_hbm,
    spatial_out_hbm,
    temporal_in_hbm,
    temporal_out_hbm,
    conv_out_hbm,
    denoised_ref,
    queue_ref,
    steps_ref,
    latents_ref,
    noise_ref,
    conv_in_ref,
    time_ref,
    spatial_in_ref,
    spatial_out_ref,
    temporal_in_ref,
    temporal_out_ref,
    conv_out_ref,
    conv_in_t,
    score_w,
    mixed_w,
    temporal_in_t,
    temporal_out_t,
    conv_out_t,
    frame_ref,
    entered_ref,
    patch_ref,
    scaled_ref,
    score_ref,
    weight_ref,
    tkv_ref,
    rows_ref,
    sent_ref,
    beside_ref,
    parts_ref,
    own_out_ref,
    next_out_ref,
    own_in_ref,
    load_sem,
    rows_send,
    rows_recv,
    beside_send,
    beside_recv,
    next_send,
    next_recv,
    own_send,
    own_recv,
):
    queue_len, row_len, comm = sizes
    channels = time_ref.shape[0]
    head_dim = channels // HEADS
    width = latents_ref.shape[3]
    pixels = row_len * width
    if comm:
        me_q = lax.axis_index("queue")
        me_r = lax.axis_index("row")
    else:
        me_q = 5
        me_r = 3
    core = lax.rem(me_q, 2)
    sibling = me_q + 1 - 2 * core
    last_frame = queue_len - 1

    def row_at(offset):
        return lax.rem(me_r + offset + row_len, row_len)

    def send(source, target, send_sem, recv_sem, device):
        return pltpu.make_async_remote_copy(
            src_ref=source,
            dst_ref=target,
            send_sem=send_sem,
            recv_sem=recv_sem,
            device_id=device,
            device_id_type=MESH,
        )

    if comm:
        barrier = pltpu.get_barrier_semaphore()

        def greet(q, r):
            pl.semaphore_signal(barrier, inc=1, device_id=(q, r), device_id_type=MESH)

        for offset in range(1, row_len):
            greet(me_q, row_at(offset))
        greet(sibling, me_r)
        for distance in (2, 4):

            @pl.when(me_q + distance <= last_frame)
            def _():
                greet(me_q + distance, me_r)

            @pl.when(me_q - distance >= 0)
            def _():
                greet(me_q - distance, me_r)

    loads = [
        pltpu.make_async_copy(source, target, load_sem.at[index])
        for index, (source, target) in enumerate(
            (
                (latents_hbm, latents_ref),
                (noise_hbm, noise_ref),
                (steps_hbm, steps_ref),
                (time_hbm, time_ref),
                (conv_in_hbm, conv_in_ref),
                (spatial_in_hbm, spatial_in_ref),
                (spatial_out_hbm, spatial_out_ref),
                (temporal_in_hbm, temporal_in_ref),
                (temporal_out_hbm, temporal_out_ref),
                (conv_out_hbm, conv_out_ref),
            )
        )
    ]
    for load in loads:
        load.start()

    loads[0].wait()
    loads[1].wait()
    latents = latents_ref[0, :, 0, :]
    empty = jnp.zeros_like(latents)
    state = jnp.concatenate([latents, empty], axis=0)
    rows_ref[me_r] = jnp.concatenate([latents, noise_ref[0, :, 0, :]], axis=0)

    loads[2].wait()
    level_now = steps_ref[0, 0].astype(F32)
    level_next = steps_ref[0, 1].astype(F32)
    signal_now, rest_now = plan(jnp.full((8, width), level_now, F32))
    signal_next, rest_next = plan(jnp.full((8, width), level_next, F32))
    keep = jnp.sqrt(signal_next) / jnp.sqrt(signal_now)
    push = jnp.sqrt(rest_next) - keep * jnp.sqrt(rest_now)

    half = channels // 2
    column = lax.broadcasted_iota(jnp.int32, (8, channels), 1)
    place = jnp.where(column < half, column, column - half).astype(F32)
    angle = level_now * jnp.exp(place * (-math.log(10000.0) / half))
    embedding = jnp.where(column < half, jnp.cos(angle), jnp.sin(angle)).astype(BF16)
    loads[3].wait()
    projected = dot(embedding, time_ref[...])
    bias = projected[0:1] / (1.0 + jnp.exp(-projected[0:1]))
    bias = bias - jnp.mean(bias, axis=1, keepdims=True)

    loads[4].wait()
    wide = conv_in_ref[...].astype(F32)
    wide = wide - jnp.mean(wide, axis=1, keepdims=True)
    gap = jnp.zeros((4, channels), F32)
    lone = jnp.concatenate([bias, gap[0:3]], axis=0)
    centred = jnp.concatenate(
        [wide[0:12], gap, wide[12:24], lone, wide[24:36], gap], axis=0
    )
    rows = centred.shape[0]
    high, low = parts_of(centred)
    conv_in_t[...] = jnp.concatenate([high, low], axis=0).astype(F32).T.astype(BF16)

    if comm:
        def reaches(space, distance):
            return lax.div(space + queue_len - distance, queue_len)

        greeted = row_len
        for space in (me_q, last_frame - me_q):
            greeted += reaches(space, 2) + reaches(space, 4)
        pl.semaphore_wait(barrier, greeted)

    row_copies = []
    if comm:
        for offset in range(1, row_len):
            copy = send(
                rows_ref.at[me_r],
                rows_ref.at[me_r],
                rows_send.at[offset],
                rows_recv.at[offset],
                (me_q, row_at(offset)),
            )
            copy.start()
            row_copies.append(copy)

    loads[5].wait()
    seen = dot(high, spatial_in_ref[...]) + dot(low, spatial_in_ref[...])
    head_of = lax.broadcasted_iota(jnp.int32, (rows, channels), 1) // head_dim

    def by_head(values, slots=False):
        pieces = []
        for head in range(HEADS):
            own = jnp.where(head_of == head, values, 0.0)
            pieces += [own, own, jnp.zeros((128 - 2 * rows, channels), F32)] if slots else [own]
        return jnp.concatenate(pieces, axis=0)

    query_high, query_low = parts_of(seen[:, :channels])
    key_high, key_low = parts_of(by_head(seen[:, channels : 2 * channels], True))
    product = (
        dot_rows(query_high, key_high)
        + dot_rows(query_low, key_high)
        + dot_rows(query_high, key_low)
    ) * (1.0 / math.sqrt(head_dim))
    high, low = parts_of(product)
    score_w[0:rows] = high
    score_w[rows : 2 * rows] = high
    score_w[2 * rows : 128] = jnp.zeros((128 - 2 * rows, HEADS * 128), BF16)
    score_w[128 : 128 + rows] = low
    loads[6].wait()
    turned = spatial_out_ref[...].T
    values = by_head(seen[:, 2 * channels :])
    value_high, value_low = parts_of(jnp.concatenate([values] * 3, axis=0))
    product = dot_rows(turned, value_high) + dot_rows(turned, value_low)
    high, low = parts_of(product)
    third = lax.broadcasted_iota(jnp.int32, product.shape, 1) // (HEADS * rows)
    mixed_w[...] = jnp.where(third < 2, high.astype(F32), low.astype(F32)).astype(BF16)

    loads[7].wait()
    temporal_in_t[...] = temporal_in_ref[...].T
    loads[8].wait()
    temporal_out_t[...] = temporal_out_ref[...].T
    loads[9].wait()
    turned = conv_out_ref[...].astype(F32)
    pieces = []
    for col_step in range(3):
        for row_step in range(3):
            base = 4 * (3 * row_step + col_step)
            pieces.append(turned[base : base + 4])
            pieces.append(gap)
    pieces.append(jnp.zeros((8, channels), F32))
    conv_out_t[...] = jnp.concatenate(pieces, axis=0).astype(BF16)
    scaled_ref[2 * rows : 2 * rows + 16, :] = jnp.ones((16, pixels), BF16)
    scaled_ref[2 * rows + 16 : 128, :] = jnp.zeros((128 - 2 * rows - 16, pixels), BF16)
    scaled_ref[128 + rows :, :] = jnp.zeros((128 - rows, pixels), BF16)

    for copy in row_copies:
        copy.wait_recv()

    own_columns = pl.ds(pl.multiple_of(me_r * width, width), width)
    sublane = lax.broadcasted_iota(jnp.int32, (8, width), 0)
    upper = sublane < 4
    constant = jnp.where(sublane == 4, 1.0, 0.0)
    unsent = list(row_copies)
    guarded_unsent = []
    own_copies = []
    middles = []
    images = []
    for y in range(row_len):
        images.append(jnp.where(upper, rows_ref[y], 0.0))
        entered_ref[y] = jnp.where(upper, pltpu.roll(rows_ref[y], 4, 0), 0.0)

    for step in range(STEPS):
        tiles = []
        for y in range(row_len):
            tile = images[y]
            tiles.append(
                jnp.concatenate(
                    [shifted(tile, 0) + pltpu.roll(tile, 4, 0), shifted(tile, 2) + constant],
                    axis=0,
                ).astype(BF16)
            )
        nothing = jnp.zeros_like(tiles[0])
        for y in range(row_len):
            for a in range(3):
                other = y + a - 1
                patch_ref[16 * a : 16 * a + 16, y * width : (y + 1) * width] = (
                    tiles[other] if 0 <= other < row_len else nothing
                )

        chunk = 2 * width
        for lower in range(0, pixels, chunk):
            span = slice(lower, lower + chunk)
            patch = patch_ref[:, span]
            hidden = dot(conv_in_t[...], jnp.concatenate([patch, patch], axis=0))
            factor = lax.rsqrt(jnp.mean(hidden * hidden, axis=0, keepdims=True) + 1e-05)
            high, low = parts_of(patch.astype(F32) * factor)
            scaled_ref[0:rows, span] = high
            scaled_ref[rows : 2 * rows, span] = low
            scaled_ref[128 : 128 + rows, span] = high

        patch = patch_ref[:, own_columns]
        hidden = dot(conv_in_t[...], jnp.concatenate([patch, patch], axis=0))
        queries = dot_columns(scaled_ref[0 : 128 + rows, own_columns], score_w[...])
        high, low = parts_of(queries)
        lefts = [
            jnp.concatenate(
                [high[:, 128 * head : 128 * head + 128], low[:, 128 * head : 128 * head + 128]],
                axis=1,
            )
            for head in range(HEADS)
        ]
        score_ref[...] = dot(jnp.concatenate(lefts, axis=0), scaled_ref[...])
        for lower in range(0, HEADS * width, 32):
            block = score_ref[lower : lower + 32, :]
            peak = jnp.max(block, axis=1, keepdims=True)
            weight_ref[lower : lower + 32, :] = jnp.exp(block - peak).astype(BF16)
        summed = dot_rows(scaled_ref[rows : 128 + rows, :], weight_ref[...])
        mixed = (summed[0:rows] + summed[128 - rows : 128]) / summed[rows : rows + 1]
        high, low = parts_of(
            jnp.concatenate(
                [mixed[:, width * head : width * (head + 1)] for head in range(HEADS)], axis=0
            )
        )
        hidden = hidden + dot(mixed_w[...], jnp.concatenate([high, low, high], axis=0))
        normed = layer_norm_columns(hidden).astype(BF16)
        sent_ref[step] = normed

        within = (
            me_q >= 2,
            me_q + 2 <= last_frame,
            me_q >= 4,
            me_q + 4 <= last_frame,
        )
        if comm:
            direct = []
            for slot, offset in enumerate((2, -2, 4, -4)):
                copy = send(
                    sent_ref.at[step],
                    beside_ref.at[step, slot],
                    beside_send.at[step, slot],
                    beside_recv.at[step, slot],
                    (me_q + offset, me_r),
                )
                direct.append(copy)
                target = me_q + offset
                reachable = jnp.logical_and(target >= 0, target <= last_frame)
                pl.when(reachable)(copy.start)
                guarded_unsent.append((reachable, copy))
            near = send(
                sent_ref.at[step],
                beside_ref.at[step, 4],
                beside_send.at[step, 4],
                beside_recv.at[step, 4],
                (sibling, me_r),
            )
            near.start()
            unsent.append(near)

        projected = dot(temporal_in_t[...], normed).astype(BF16).astype(F32)
        tqueries = projected[:channels] * (1.0 / math.sqrt(head_dim))
        tkv_ref[2 * HALF] = projected[2 * channels :]
        scores = [None] * SPAN

        def score_of(keys):
            return jnp.concatenate(
                [
                    jnp.sum(
                        tqueries[h * head_dim : (h + 1) * head_dim]
                        * keys[h * head_dim : (h + 1) * head_dim],
                        axis=0,
                        keepdims=True,
                    )
                    for h in range(HEADS)
                ],
                axis=0,
            )

        def take(slots):
            joined = [beside_ref[step, slot] for slot in slots]
            joined = joined[0] if len(slots) == 1 else jnp.concatenate(joined, axis=1)
            projected = dot(temporal_in_t[channels:, :], joined).astype(BF16).astype(F32)
            for inner, slot in enumerate(slots):
                part = projected[:, inner * width : (inner + 1) * width]
                scores[slot] = score_of(part[:channels])
                tkv_ref[slot] = part[channels:]

        scores[2 * HALF] = score_of(projected[channels : 2 * channels])
        far = 3 - core
        outer = 2 + core
        far_within = jnp.where(core == 0, me_q + 4, queue_len + 3 - me_q) <= last_frame
        outer_within = jnp.where(core == 0, me_q, last_frame - me_q) >= 4
        if comm:
            near.wait_recv()
        take([4])
        if comm:

            def received(slot, good):
                copy = send(
                    sent_ref.at[step],
                    beside_ref.at[step, slot],
                    beside_send.at[step, slot],
                    beside_recv.at[step, slot],
                    (sibling, me_r),
                )
                pl.when(good)(copy.wait_recv)

                @pl.when(jnp.logical_not(good))
                def _():
                    beside_ref[step, slot] = jnp.zeros((channels, width), BF16)

            def forward(slot, target, good):
                received(slot, good)
                copy = send(
                    beside_ref.at[step, slot],
                    beside_ref.at[step, target],
                    beside_send.at[step, target],
                    beside_recv.at[step, target],
                    (sibling, me_r),
                )
                copy.start()
                unsent.append(copy)
                return copy

            third = forward(far, 7, far_within)
            received(outer, outer_within)
        take([2, 3])
        if comm:
            first = forward(0, 5, within[0])
            second = forward(1, 6, within[1])
        take([0, 1])
        if comm:
            first.wait_recv()
            third.wait_recv()
        take([5, 7])
        if comm:
            second.wait_recv()
        take([6])

        away = sibling - me_q
        frames = (
            me_q - 2,
            me_q + 2,
            me_q - 4,
            me_q + 4,
            sibling,
            sibling - 2,
            sibling + 2,
            me_q - 3 * away,
        )
        for slot, frame in enumerate(frames):
            good = jnp.logical_and(frame >= 0, frame <= last_frame)
            scores[slot] = jnp.where(good, scores[slot], -jnp.inf)
        peak = functools.reduce(jnp.maximum, scores)
        weights = [jnp.exp(score - peak) for score in scores]
        total = functools.reduce(jnp.add, weights)
        rounded = [weight.astype(BF16).astype(F32) for weight in weights]
        mixed = []
        for head in range(HEADS):
            blended = None
            for index in range(SPAN):
                term = (
                    rounded[index][head : head + 1]
                    * tkv_ref[index, head * head_dim : (head + 1) * head_dim, :]
                )
                blended = term if blended is None else blended + term
            mixed.append(blended / total[head : head + 1])
        mixed = jnp.concatenate(mixed, axis=0).astype(BF16)
        hidden = hidden + dot(temporal_out_t[...], mixed)
        normed = layer_norm_columns(hidden).astype(BF16)

        taps = dot(conv_out_t[...], normed)
        added = shifted(taps[0:24], 0) + taps[24:48] + shifted(taps[48:72], 2)
        below = push * added[0:8]
        middle = push * added[8:16] + keep * state
        above = push * added[16:24]
        middles.append(middle)
        own_out_ref[step, 0] = below
        own_out_ref[step, 1] = above
        next_out_ref[step, 0:8] = middle
        next_out_ref[step, 8:16] = below + pltpu.roll(above, 4, 0)

        last = step == STEPS - 1
        next_copies = []
        if comm:
            for offset in (0, 1, row_len - 1) if last else range(row_len):
                copy = send(
                    next_out_ref.at[step],
                    parts_ref.at[step, me_r],
                    next_send.at[step, offset],
                    next_recv.at[step, offset],
                    (me_q - 1, row_at(offset)),
                )
                pl.when(me_q > 0)(copy.start)
                guarded_unsent.append((me_q > 0, copy))
                next_copies.append(copy)
            for slot, offset in enumerate((1, -1)):
                copy = send(
                    own_out_ref.at[step, slot],
                    own_in_ref.at[step, slot],
                    own_send.at[step, slot],
                    own_recv.at[step, slot],
                    (me_q, row_at(offset)),
                )
                copy.start()
                own_copies.append(copy)
            for copy in next_copies:
                pl.when(me_q < last_frame)(copy.wait_recv)
        entering = me_q == last_frame
        if not last:
            images = []
            for y in range(row_len):
                total = parts_ref[step, y, 0:8]
                if y > 0:
                    total = total + parts_ref[step, y - 1, 8:16]
                if y < row_len - 1:
                    total = total + pltpu.roll(parts_ref[step, y + 1, 8:16], 4, 0)
                total = jnp.where(entering, entered_ref[y], jnp.where(upper, total, 0.0))
                images.append(total)
                frame_ref[y] = total
            state = frame_ref[me_r]
        else:
            total = parts_ref[step, me_r, 0:8]
            total = total + jnp.where(me_r == 0, 0.0, parts_ref[step, row_at(-1), 8:16])
            total = total + jnp.where(
                me_r == row_len - 1, 0.0, pltpu.roll(parts_ref[step, row_at(1), 8:16], 4, 0)
            )
            queue_ref[0, :, 0, :] = jnp.where(entering, noise_ref[step, :, 0, :], total[0:4])

    for copy in own_copies:
        copy.wait()
    for step in range(STEPS):
        total = middles[step]
        total = total + jnp.where(me_r == 0, 0.0, own_in_ref[step, 0])
        total = total + jnp.where(me_r == row_len - 1, 0.0, own_in_ref[step, 1])
        denoised_ref[step, 0, :, 0, :] = total[0:4]
    for copy in unsent:
        copy.wait_send()
    for reachable, copy in guarded_unsent:
        pl.when(reachable)(copy.wait_send)


def on_device(
    latents,
    fresh_noise,
    timesteps,
    conv_in_w,
    time_w,
    spatial_in,
    spatial_out,
    temporal_in,
    temporal_out,
    conv_out_w,
    *,
    sizes,
):
    queue_len, row_len, comm = sizes
    channels = conv_in_w.shape[1]
    width = latents.shape[3]
    pixels = row_len * width
    vmem = pl.BlockSpec(memory_space=pltpu.VMEM)
    hbm = pl.BlockSpec(memory_space=pl.ANY)
    dma = pltpu.SemaphoreType.DMA
    weights = (conv_in_w, time_w, spatial_in, spatial_out, temporal_in, temporal_out, conv_out_w.T)
    arguments = (timesteps, latents, fresh_noise) + weights
    return pl.pallas_call(
        functools.partial(kernel, sizes),
        out_shape=(
            jax.ShapeDtypeStruct((STEPS,) + latents.shape, F32),
            jax.ShapeDtypeStruct(latents.shape, F32),
        ),
        in_specs=[hbm] * len(arguments),
        out_specs=(vmem, vmem),
        scratch_shapes=[pltpu.SMEM(timesteps.shape, timesteps.dtype)]
        + [pltpu.VMEM(array.shape, array.dtype) for array in arguments[1:]]
        + [
            pltpu.VMEM((channels, 96), BF16),
            pltpu.VMEM((176, HEADS * 128), BF16),
            pltpu.VMEM((channels, 3 * HEADS * 48), BF16),
            pltpu.VMEM((3 * channels, channels), BF16),
            pltpu.VMEM((channels, channels), BF16),
            pltpu.VMEM((80, channels), BF16),
            pltpu.VMEM((row_len, 8, width), F32),
            pltpu.VMEM((row_len, 8, width), F32),
            pltpu.VMEM((48, pixels), BF16),
            pltpu.VMEM((256, pixels), BF16),
            pltpu.VMEM((HEADS * width, pixels), F32),
            pltpu.VMEM((HEADS * width, pixels), BF16),
            pltpu.VMEM((SPAN, channels, width), F32),
            pltpu.VMEM((row_len, 8, width), F32),
            pltpu.VMEM((STEPS, channels, width), BF16),
            pltpu.VMEM((STEPS, 2 * HALF, channels, width), BF16),
            pltpu.VMEM((STEPS, row_len, 16, width), F32),
            pltpu.VMEM((STEPS, 2, 8, width), F32),
            pltpu.VMEM((STEPS, 16, width), F32),
            pltpu.VMEM((STEPS, 2, 8, width), F32),
            dma((len(arguments),)),
            dma((row_len,)),
            dma((row_len,)),
            dma((STEPS, 2 * HALF)),
            dma((STEPS, 2 * HALF)),
            dma((STEPS, row_len)),
            dma((STEPS, row_len)),
            dma((STEPS, 2)),
            dma((STEPS, 2)),
        ],
        compiler_params=pltpu.CompilerParams(
            collective_id=0 if comm else None,
            has_side_effects=True,
            vmem_limit_bytes=40 * 1024 * 1024,
        ),
        name="denoise",
    )(*(pltpu.with_memory_space_constraint(array, pltpu.HBM) for array in arguments))


def solution(mesh):
    sizes = (mesh.shape["queue"], mesh.shape["row"], True)
    return jax.shard_map(
        functools.partial(on_device, sizes=sizes),
        mesh=mesh,
        in_specs=(
            P("queue", None, "row", None),
            P(None, None, "row", None),
            P("queue", None),
            P(),
            P(),
            P(),
            P(),
            P(),
            P(),
            P(),
        ),
        out_specs=(P(None, "queue", None, "row", None), P("queue", None, "row", None)),
        check_vma=False,
    )
```

```python
import functools
import math

import jax
import jax.numpy as jnp
from jax import lax
from jax.experimental import pallas as pl
from jax.experimental.pallas import tpu as pltpu
from jax.sharding import PartitionSpec as P

HEADS = 5
HALF = 4
STEPS = 2
SPAN = 2 * HALF + 1
F32 = jnp.float32
BF16 = jnp.bfloat16
MESH = pl.DeviceIdType.MESH


def dot(left, right):
    return jnp.dot(left, right, preferred_element_type=F32)


def dot_rows(left, right):
    return lax.dot_general(left, right, (((1,), (1,)), ((), ())), preferred_element_type=F32)


def dot_columns(left, right):
    return lax.dot_general(left, right, (((0,), (0,)), ((), ())), preferred_element_type=F32)


def parts_of(values):
    high = values.astype(BF16)
    return high, (values - high.astype(F32)).astype(BF16)


def plan(level):
    start = 0.008 / 1.008 * math.pi / 2.0
    base = math.cos(start) ** 2
    angle = ((level + 1.0) / 1000.0 + 0.008) / 1.008 * (math.pi / 2.0)
    signal = jnp.cos(angle) ** 2 / base
    remain = jnp.sin(angle - start) * jnp.sin(angle + start) / base
    return (signal, remain)


def shifted(tile, step):
    if step == 1:
        return tile
    width = tile.shape[1]
    lane = lax.broadcasted_iota(jnp.int32, tile.shape, 1)
    if step == 0:
        return jnp.where(lane == 0, 0.0, pltpu.roll(tile, 1, 1))
    return jnp.where(lane == width - 1, 0.0, pltpu.roll(tile, width - 1, 1))


def layer_norm_columns(values):
    centre = values - jnp.mean(values, axis=0, keepdims=True)
    return centre * lax.rsqrt(jnp.mean(centre * centre, axis=0, keepdims=True) + 1e-05)


def turned_rows(tile, step):
    return jnp.concatenate([tile[8 - step :], tile[: 8 - step]], axis=0) if step else tile


def compact(blocks):
    row = lax.broadcasted_iota(jnp.int32, (8, blocks[0].shape[1]), 0)
    pieces = []
    lasts = []
    constants = None
    for index, block in enumerate(blocks):
        tiles = [block[8 * i : 8 * i + 8] for i in range(6)]
        pieces += [tiles[0], tiles[2], tiles[4]]
        odd = [jnp.where(row < 4, tiles[i], 0.0) for i in (1, 3, 5)]
        pieces.append(odd[0] + turned_rows(odd[1], 4))
        lasts.append(odd[2])
        constant = turned_rows(jnp.where(row == 4, tiles[3], 0.0), (index + 4) % 8)
        constants = constant if constants is None else constants + constant
    for first in range(0, len(blocks), 2):
        pieces.append(lasts[first] + turned_rows(lasts[first + 1], 4))
    return jnp.concatenate(pieces + [constants], axis=0)


def kernel(
    sizes,
    steps_hbm,
    latents_hbm,
    noise_hbm,
    conv_in_hbm,
    time_hbm,
    spatial_in_hbm,
    spatial_out_hbm,
    temporal_in_hbm,
    temporal_out_hbm,
    conv_out_hbm,
    denoised_ref,
    queue_ref,
    steps_ref,
    latents_ref,
    noise_ref,
    conv_in_ref,
    time_ref,
    spatial_in_ref,
    spatial_out_ref,
    temporal_in_ref,
    temporal_out_ref,
    conv_out_ref,
    conv_in_t,
    score_w,
    mixed_w,
    temporal_in_t,
    temporal_out_t,
    conv_out_t,
    common_w,
    frame_ref,
    entered_ref,
    patch_ref,
    scaled_ref,
    score_ref,
    weight_ref,
    tkv_ref,
    rows_ref,
    sent_ref,
    beside_ref,
    factor_sent_ref,
    factor_ref,
    own_lean_ref,
    lean_ref,
    parts_ref,
    own_out_ref,
    next_out_ref,
    own_in_ref,
    load_sem,
    rows_send,
    rows_recv,
    beside_send,
    beside_recv,
    factor_send,
    factor_recv,
    lean_send,
    lean_recv,
    next_send,
    next_recv,
    own_send,
    own_recv,
):
    queue_len, row_len, comm = sizes
    channels = time_ref.shape[0]
    head_dim = channels // HEADS
    width = latents_ref.shape[3]
    pixels = row_len * width
    if comm:
        me_q = lax.axis_index("queue")
        me_r = lax.axis_index("row")
    else:
        me_q = 5
        me_r = 3
    core = lax.rem(me_q, 2)
    sibling = me_q + 1 - 2 * core
    last_frame = queue_len - 1

    def row_at(offset):
        return lax.rem(me_r + offset + row_len, row_len)

    def send(source, target, send_sem, recv_sem, device):
        return pltpu.make_async_remote_copy(
            src_ref=source,
            dst_ref=target,
            send_sem=send_sem,
            recv_sem=recv_sem,
            device_id=device,
            device_id_type=MESH,
        )

    if comm:
        barrier = pltpu.get_barrier_semaphore()

        def greet(q, r):
            pl.semaphore_signal(barrier, inc=1, device_id=(q, r), device_id_type=MESH)

        for offset in range(1, row_len):
            greet(me_q, row_at(offset))
        greet(sibling, me_r)
        for distance in (2, 4):

            @pl.when(me_q + distance <= last_frame)
            def _():
                greet(me_q + distance, me_r)

            @pl.when(me_q - distance >= 0)
            def _():
                greet(me_q - distance, me_r)

    loads = [
        pltpu.make_async_copy(source, target, load_sem.at[index])
        for index, (source, target) in enumerate(
            (
                (latents_hbm, latents_ref),
                (noise_hbm, noise_ref),
                (steps_hbm, steps_ref),
                (time_hbm, time_ref),
                (conv_in_hbm, conv_in_ref),
                (spatial_in_hbm, spatial_in_ref),
                (spatial_out_hbm, spatial_out_ref),
                (temporal_in_hbm, temporal_in_ref),
                (temporal_out_hbm, temporal_out_ref),
                (conv_out_hbm, conv_out_ref),
            )
        )
    ]
    for load in loads:
        load.start()

    loads[0].wait()
    loads[1].wait()
    latents = latents_ref[0, :, 0, :]
    empty = jnp.zeros_like(latents)
    state = jnp.concatenate([latents, empty], axis=0)
    rows_ref[me_r] = jnp.concatenate([latents, noise_ref[0, :, 0, :]], axis=0)

    loads[2].wait()
    level_now = steps_ref[0, 0].astype(F32)
    level_next = steps_ref[0, 1].astype(F32)
    signal_now, rest_now = plan(jnp.full((8, width), level_now, F32))
    signal_next, rest_next = plan(jnp.full((8, width), level_next, F32))
    keep = jnp.sqrt(signal_next) / jnp.sqrt(signal_now)
    push = jnp.sqrt(rest_next) - keep * jnp.sqrt(rest_now)

    half = channels // 2
    column = lax.broadcasted_iota(jnp.int32, (8, channels), 1)
    place = jnp.where(column < half, column, column - half).astype(F32)
    angle = level_now * jnp.exp(place * (-math.log(10000.0) / half))
    embedding = jnp.where(column < half, jnp.cos(angle), jnp.sin(angle)).astype(BF16)
    loads[3].wait()
    projected = dot(embedding, time_ref[...])
    bias = projected[0:1] / (1.0 + jnp.exp(-projected[0:1]))
    bias = bias - jnp.mean(bias, axis=1, keepdims=True)

    loads[4].wait()
    wide = conv_in_ref[...].astype(F32)
    wide = wide - jnp.mean(wide, axis=1, keepdims=True)
    gap = jnp.zeros((4, channels), F32)
    lone = jnp.concatenate([bias, gap[0:3]], axis=0)
    centred = jnp.concatenate(
        [wide[0:12], gap, wide[12:24], lone, wide[24:36], gap], axis=0
    )
    rows = centred.shape[0]
    high, low = parts_of(centred)
    conv_in_t[...] = jnp.concatenate([high, low], axis=0).astype(F32).T.astype(BF16)

    if comm:
        def reaches(space, distance):
            return lax.div(space + queue_len - distance, queue_len)

        greeted = row_len
        for space in (me_q, last_frame - me_q):
            greeted += reaches(space, 2) + reaches(space, 4)
        pl.semaphore_wait(barrier, greeted)

    row_copies = []
    if comm:
        for offset in range(1, row_len):
            copy = send(
                rows_ref.at[me_r],
                rows_ref.at[me_r],
                rows_send.at[offset],
                rows_recv.at[offset],
                (me_q, row_at(offset)),
            )
            copy.start()
            row_copies.append(copy)

    loads[5].wait()
    seen = dot(high, spatial_in_ref[...]) + dot(low, spatial_in_ref[...])
    head_of = lax.broadcasted_iota(jnp.int32, (rows, channels), 1) // head_dim

    def by_head(values, slots=False):
        pieces = []
        for head in range(HEADS):
            own = jnp.where(head_of == head, values, 0.0)
            pieces += [own, own, jnp.zeros((128 - 2 * rows, channels), F32)] if slots else [own]
        return jnp.concatenate(pieces, axis=0)

    query_high, query_low = parts_of(seen[:, :channels])
    key_high, key_low = parts_of(by_head(seen[:, channels : 2 * channels], True))
    product = (
        dot_rows(query_high, key_high)
        + dot_rows(query_low, key_high)
        + dot_rows(query_high, key_low)
    ) * (1.0 / math.sqrt(head_dim))
    high, low = parts_of(product)
    score_w[0:rows] = high
    score_w[rows : 2 * rows] = high
    score_w[2 * rows : 128] = jnp.zeros((128 - 2 * rows, HEADS * 128), BF16)
    score_w[128 : 128 + rows] = low
    loads[6].wait()
    turned = spatial_out_ref[...].T
    values = by_head(seen[:, 2 * channels :])
    value_high, value_low = parts_of(jnp.concatenate([values] * 3, axis=0))
    product = dot_rows(turned, value_high) + dot_rows(turned, value_low)
    product = product - jnp.mean(product, axis=0, keepdims=True)
    high, low = parts_of(product)
    third = lax.broadcasted_iota(jnp.int32, product.shape, 1) // (HEADS * rows)
    mixed_w[...] = jnp.where(third < 2, high.astype(F32), low.astype(F32)).astype(BF16)

    loads[7].wait()
    value_high, value_low = parts_of(values)
    product = dot(value_high, spatial_out_ref[...]) + dot(value_low, spatial_out_ref[...])
    wide = compact([centred] + [product[rows * h : rows * (h + 1)] for h in range(HEADS)])
    wide = wide - jnp.mean(wide, axis=1, keepdims=True)
    high, low = parts_of(wide)
    product = dot(high, temporal_in_ref[:, channels:]) + dot(low, temporal_in_ref[:, channels:])
    sides = lax.broadcasted_iota(jnp.int32, product.shape, 0) < 216
    common_w[...] = jnp.where(sides, product, 0.0).T.astype(BF16)
    own_lean_ref[...] = jnp.where(sides, 0.0, product)[208:224].astype(BF16)

    within = (
        me_q >= 2,
        me_q + 2 <= last_frame,
        me_q >= 4,
        me_q + 4 <= last_frame,
    )
    unsent = list(row_copies)
    guarded_unsent = []

    def scatter(source, targets, send_sems, recv_sems):
        for slot, offset in enumerate((2, -2, 4, -4)):
            target = me_q + offset
            copy = send(
                source,
                targets.at[slot],
                send_sems.at[slot],
                recv_sems.at[slot],
                (target, me_r),
            )
            reachable = jnp.logical_and(target >= 0, target <= last_frame)
            pl.when(reachable)(copy.start)
            guarded_unsent.append((reachable, copy))
        copy = send(source, targets.at[4], send_sems.at[4], recv_sems.at[4], (sibling, me_r))
        copy.start()
        unsent.append(copy)
        return copy

    def relay(slot, target, targets, send_sems, recv_sems):
        copy = send(
            targets.at[slot],
            targets.at[target],
            send_sems.at[target],
            recv_sems.at[target],
            (sibling, me_r),
        )
        copy.start()
        unsent.append(copy)
        return copy

    def arrived(slot, good, targets, send_sems, recv_sems):
        copy = send(
            targets.at[slot], targets.at[slot], send_sems.at[slot], recv_sems.at[slot], (sibling, me_r)
        )
        pl.when(good)(copy.wait_recv)

        @pl.when(jnp.logical_not(good))
        def _():
            targets[slot] = jnp.zeros(targets.shape[1:], targets.dtype)

    if comm:
        leans = (lean_ref, lean_send, lean_recv)
        near_lean = scatter(own_lean_ref, *leans)

    temporal_in_t[...] = temporal_in_ref[...].T
    loads[8].wait()
    temporal_out_t[...] = temporal_out_ref[...].T
    loads[9].wait()
    turned = conv_out_ref[...].astype(F32)
    pieces = []
    for col_step in range(3):
        for row_step in range(3):
            base = 4 * (3 * row_step + col_step)
            pieces.append(turned[base : base + 4])
            pieces.append(gap)
    pieces.append(jnp.zeros((8, channels), F32))
    conv_out_t[...] = jnp.concatenate(pieces, axis=0).astype(BF16)
    scaled_ref[2 * rows : 2 * rows + 16, :] = jnp.ones((16, pixels), BF16)
    scaled_ref[2 * rows + 16 : 128, :] = jnp.zeros((128 - 2 * rows - 16, pixels), BF16)
    scaled_ref[128 + rows :, :] = jnp.zeros((128 - rows, pixels), BF16)

    for copy in row_copies:
        copy.wait_recv()

    own_columns = pl.ds(pl.multiple_of(me_r * width, width), width)
    sublane = lax.broadcasted_iota(jnp.int32, (8, width), 0)
    upper = sublane < 4
    constant = jnp.where(sublane == 4, 1.0, 0.0)
    own_copies = []
    middles = []
    images = []
    for y in range(row_len):
        images.append(jnp.where(upper, rows_ref[y], 0.0))
        entered_ref[y] = jnp.where(upper, pltpu.roll(rows_ref[y], 4, 0), 0.0)

    for step in range(STEPS):
        tiles = []
        for y in range(row_len):
            tile = images[y]
            tiles.append(
                jnp.concatenate(
                    [shifted(tile, 0) + pltpu.roll(tile, 4, 0), shifted(tile, 2) + constant],
                    axis=0,
                ).astype(BF16)
            )
        nothing = jnp.zeros_like(tiles[0])
        for y in range(row_len):
            for a in range(3):
                other = y + a - 1
                patch_ref[16 * a : 16 * a + 16, y * width : (y + 1) * width] = (
                    tiles[other] if 0 <= other < row_len else nothing
                )

        chunk = 2 * width
        for lower in range(0, pixels, chunk):
            span = slice(lower, lower + chunk)
            patch = patch_ref[:, span]
            hidden = dot(conv_in_t[...], jnp.concatenate([patch, patch], axis=0))
            factor = lax.rsqrt(jnp.mean(hidden * hidden, axis=0, keepdims=True) + 1e-05)
            high, low = parts_of(patch.astype(F32) * factor)
            scaled_ref[0:rows, span] = high
            scaled_ref[rows : 2 * rows, span] = low
            scaled_ref[128 : 128 + rows, span] = high

        patch = patch_ref[:, own_columns]
        hidden = dot(conv_in_t[...], jnp.concatenate([patch, patch], axis=0))
        queries = dot_columns(scaled_ref[0 : 128 + rows, own_columns], score_w[...])
        high, low = parts_of(queries)
        lefts = [
            jnp.concatenate(
                [high[:, 128 * head : 128 * head + 128], low[:, 128 * head : 128 * head + 128]],
                axis=1,
            )
            for head in range(HEADS)
        ]
        groups = ((0, 2), (2, 4), (4, 5))
        for first, after in groups:
            score_ref[first * width : after * width, :] = dot(
                jnp.concatenate(lefts[first:after], axis=0), scaled_ref[...]
            )
        summed = []
        for first, after in groups:
            for lower in range(first * width, after * width, 32):
                block = score_ref[lower : lower + 32, :]
                peak = jnp.max(block, axis=1, keepdims=True)
                weight_ref[lower : lower + 32, :] = jnp.exp(block - peak).astype(BF16)
            summed.append(
                dot_rows(
                    scaled_ref[rows : 128 + rows, :], weight_ref[first * width : after * width, :]
                )
            )
        summed = jnp.concatenate(summed, axis=1)
        mixed = (summed[0:rows] + summed[128 - rows : 128]) / summed[rows : rows + 1]
        mixed = [mixed[:, width * head : width * (head + 1)] for head in range(HEADS)]
        sent_ref[step] = compact([patch.astype(F32)] + mixed).astype(BF16)
        if comm:
            groups = [
                tuple(ref.at[step] for ref in (beside_ref, beside_send, beside_recv)),
                tuple(ref.at[step] for ref in (factor_ref, factor_send, factor_recv)),
            ]
            nears = [scatter(sent_ref.at[step], *groups[0])]
        high, low = parts_of(jnp.concatenate(mixed, axis=0))
        hidden = hidden + dot(mixed_w[...], jnp.concatenate([high, low, high], axis=0))
        factor = lax.rsqrt(jnp.mean(hidden * hidden, axis=0, keepdims=True) + 1e-05)
        factor_sent_ref[step] = jnp.broadcast_to(factor, (8, width))
        if comm:
            nears.append(scatter(factor_sent_ref.at[step], *groups[1]))
            if step == 0:
                groups.append(leans)
                nears.append(near_lean)
        normed = (hidden * factor).astype(BF16)

        projected = dot(temporal_in_t[...], normed).astype(BF16).astype(F32)
        tqueries = projected[:channels] * (1.0 / math.sqrt(head_dim))
        tkv_ref[2 * HALF] = projected[2 * channels :]
        scores = [None] * SPAN

        def score_of(keys):
            return jnp.concatenate(
                [
                    jnp.sum(
                        tqueries[h * head_dim : (h + 1) * head_dim]
                        * keys[h * head_dim : (h + 1) * head_dim],
                        axis=0,
                        keepdims=True,
                    )
                    for h in range(HEADS)
                ],
                axis=0,
            )

        def take(slots):
            joined = [beside_ref[step, slot] for slot in slots]
            joined = joined[0] if len(slots) == 1 else jnp.concatenate(joined, axis=1)
            projected = dot(common_w[...], joined)
            for inner, slot in enumerate(slots):
                part = projected[:, inner * width : (inner + 1) * width]
                part = part + dot_columns(lean_ref[slot], beside_ref[step, slot, 208:224, :])
                part = (part * factor_ref[step, slot, 0:1, :]).astype(BF16).astype(F32)
                scores[slot] = score_of(part[:channels])
                tkv_ref[slot] = part[channels:]

        scores[2 * HALF] = score_of(projected[channels : 2 * channels])
        far = 3 - core
        outer = 2 + core
        far_within = jnp.where(core == 0, me_q + 4, queue_len + 3 - me_q) <= last_frame
        outer_within = jnp.where(core == 0, me_q, last_frame - me_q) >= 4
        if comm:
            for copy in nears:
                copy.wait_recv()
        take([4])
        if comm:

            def received(slot, good):
                for group in groups:
                    arrived(slot, good, *group)

            def forward(slot, target, good):
                copies = []
                for group in groups[::-1]:
                    arrived(slot, good, *group)
                    copies.append(relay(slot, target, *group))
                return copies

            def finish(copies):
                for copy in copies:
                    copy.wait_recv()

            third = forward(far, 7, far_within)
            received(outer, outer_within)
        take([2, 3])
        if comm:
            first = forward(0, 5, within[0])
            second = forward(1, 6, within[1])
        take([0, 1])
        if comm:
            finish(first)
            finish(third)
        take([5, 7])
        if comm:
            finish(second)
        take([6])

        away = sibling - me_q
        frames = (
            me_q - 2,
            me_q + 2,
            me_q - 4,
            me_q + 4,
            sibling,
            sibling - 2,
            sibling + 2,
            me_q - 3 * away,
        )
        for slot, frame in enumerate(frames):
            good = jnp.logical_and(frame >= 0, frame <= last_frame)
            scores[slot] = jnp.where(good, scores[slot], -jnp.inf)
        peak = functools.reduce(jnp.maximum, scores)
        weights = [jnp.exp(score - peak) for score in scores]
        total = functools.reduce(jnp.add, weights)
        rounded = [weight.astype(BF16).astype(F32) for weight in weights]
        mixed = []
        for head in range(HEADS):
            blended = None
            for index in range(SPAN):
                term = (
                    rounded[index][head : head + 1]
                    * tkv_ref[index, head * head_dim : (head + 1) * head_dim, :]
                )
                blended = term if blended is None else blended + term
            mixed.append(blended / total[head : head + 1])
        mixed = jnp.concatenate(mixed, axis=0).astype(BF16)
        hidden = hidden + dot(temporal_out_t[...], mixed)
        normed = layer_norm_columns(hidden).astype(BF16)

        taps = dot(conv_out_t[...], normed)
        added = shifted(taps[0:24], 0) + taps[24:48] + shifted(taps[48:72], 2)
        below = push * added[0:8]
        middle = push * added[8:16] + keep * state
        above = push * added[16:24]
        middles.append(middle)
        own_out_ref[step, 0] = below
        own_out_ref[step, 1] = above
        next_out_ref[step, 0:8] = middle
        next_out_ref[step, 8:16] = below + pltpu.roll(above, 4, 0)

        last = step == STEPS - 1
        next_copies = []
        if comm:
            for offset in (0, 1, row_len - 1) if last else range(row_len):
                copy = send(
                    next_out_ref.at[step],
                    parts_ref.at[step, me_r],
                    next_send.at[step, offset],
                    next_recv.at[step, offset],
                    (me_q - 1, row_at(offset)),
                )
                pl.when(me_q > 0)(copy.start)
                guarded_unsent.append((me_q > 0, copy))
                next_copies.append(copy)
            for slot, offset in enumerate((1, -1)):
                copy = send(
                    own_out_ref.at[step, slot],
                    own_in_ref.at[step, slot],
                    own_send.at[step, slot],
                    own_recv.at[step, slot],
                    (me_q, row_at(offset)),
                )
                copy.start()
                own_copies.append(copy)
            for copy in next_copies:
                pl.when(me_q < last_frame)(copy.wait_recv)
        entering = me_q == last_frame
        if not last:
            images = []
            for y in range(row_len):
                total = parts_ref[step, y, 0:8]
                if y > 0:
                    total = total + parts_ref[step, y - 1, 8:16]
                if y < row_len - 1:
                    total = total + pltpu.roll(parts_ref[step, y + 1, 8:16], 4, 0)
                total = jnp.where(entering, entered_ref[y], jnp.where(upper, total, 0.0))
                images.append(total)
                frame_ref[y] = total
            state = frame_ref[me_r]
        else:
            total = parts_ref[step, me_r, 0:8]
            total = total + jnp.where(me_r == 0, 0.0, parts_ref[step, row_at(-1), 8:16])
            total = total + jnp.where(
                me_r == row_len - 1, 0.0, pltpu.roll(parts_ref[step, row_at(1), 8:16], 4, 0)
            )
            queue_ref[0, :, 0, :] = jnp.where(entering, noise_ref[step, :, 0, :], total[0:4])

    for copy in own_copies:
        copy.wait()
    for step in range(STEPS):
        total = middles[step]
        total = total + jnp.where(me_r == 0, 0.0, own_in_ref[step, 0])
        total = total + jnp.where(me_r == row_len - 1, 0.0, own_in_ref[step, 1])
        denoised_ref[step, 0, :, 0, :] = total[0:4]
    for copy in unsent:
        copy.wait_send()
    for reachable, copy in guarded_unsent:
        pl.when(reachable)(copy.wait_send)


def on_device(
    latents,
    fresh_noise,
    timesteps,
    conv_in_w,
    time_w,
    spatial_in,
    spatial_out,
    temporal_in,
    temporal_out,
    conv_out_w,
    *,
    sizes,
):
    queue_len, row_len, comm = sizes
    channels = conv_in_w.shape[1]
    width = latents.shape[3]
    pixels = row_len * width
    vmem = pl.BlockSpec(memory_space=pltpu.VMEM)
    hbm = pl.BlockSpec(memory_space=pl.ANY)
    dma = pltpu.SemaphoreType.DMA
    weights = (conv_in_w, time_w, spatial_in, spatial_out, temporal_in, temporal_out, conv_out_w.T)
    arguments = (timesteps, latents, fresh_noise) + weights
    return pl.pallas_call(
        functools.partial(kernel, sizes),
        out_shape=(
            jax.ShapeDtypeStruct((STEPS,) + latents.shape, F32),
            jax.ShapeDtypeStruct(latents.shape, F32),
        ),
        in_specs=[hbm] * len(arguments),
        out_specs=(vmem, vmem),
        scratch_shapes=[pltpu.SMEM(timesteps.shape, timesteps.dtype)]
        + [pltpu.VMEM(array.shape, array.dtype) for array in arguments[1:]]
        + [
            pltpu.VMEM((channels, 96), BF16),
            pltpu.VMEM((176, HEADS * 128), BF16),
            pltpu.VMEM((channels, 3 * HEADS * 48), BF16),
            pltpu.VMEM((3 * channels, channels), BF16),
            pltpu.VMEM((channels, channels), BF16),
            pltpu.VMEM((80, channels), BF16),
            pltpu.VMEM((2 * channels, 224), BF16),
            pltpu.VMEM((row_len, 8, width), F32),
            pltpu.VMEM((row_len, 8, width), F32),
            pltpu.VMEM((48, pixels), BF16),
            pltpu.VMEM((256, pixels), BF16),
            pltpu.VMEM((HEADS * width, pixels), F32),
            pltpu.VMEM((HEADS * width, pixels), BF16),
            pltpu.VMEM((SPAN, channels, width), F32),
            pltpu.VMEM((row_len, 8, width), F32),
            pltpu.VMEM((STEPS, 224, width), BF16),
            pltpu.VMEM((STEPS, 2 * HALF, 224, width), BF16),
            pltpu.VMEM((STEPS, 8, width), F32),
            pltpu.VMEM((STEPS, 2 * HALF, 8, width), F32),
            pltpu.VMEM((16, 2 * channels), BF16),
            pltpu.VMEM((2 * HALF, 16, 2 * channels), BF16),
            pltpu.VMEM((STEPS, row_len, 16, width), F32),
            pltpu.VMEM((STEPS, 2, 8, width), F32),
            pltpu.VMEM((STEPS, 16, width), F32),
            pltpu.VMEM((STEPS, 2, 8, width), F32),
            dma((len(arguments),)),
            dma((row_len,)),
            dma((row_len,)),
            dma((STEPS, 2 * HALF)),
            dma((STEPS, 2 * HALF)),
            dma((STEPS, 2 * HALF)),
            dma((STEPS, 2 * HALF)),
            dma((2 * HALF,)),
            dma((2 * HALF,)),
            dma((STEPS, row_len)),
            dma((STEPS, row_len)),
            dma((STEPS, 2)),
            dma((STEPS, 2)),
        ],
        compiler_params=pltpu.CompilerParams(
            collective_id=0 if comm else None,
            has_side_effects=True,
            vmem_limit_bytes=40 * 1024 * 1024,
        ),
        name="denoise",
    )(*(pltpu.with_memory_space_constraint(array, pltpu.HBM) for array in arguments))


def solution(mesh):
    sizes = (mesh.shape["queue"], mesh.shape["row"], True)
    return jax.shard_map(
        functools.partial(on_device, sizes=sizes),
        mesh=mesh,
        in_specs=(
            P("queue", None, "row", None),
            P(None, None, "row", None),
            P("queue", None),
            P(),
            P(),
            P(),
            P(),
            P(),
            P(),
            P(),
        ),
        out_specs=(P(None, "queue", None, "row", None), P("queue", None, "row", None)),
        check_vma=False,
    )
```

```python
import functools
import math

import jax
import jax.numpy as jnp
from jax import lax
from jax.experimental import pallas as pl
from jax.experimental.pallas import tpu as pltpu
from jax.sharding import PartitionSpec as P

HEADS = 5
HALF = 4
STEPS = 2
SPAN = 2 * HALF + 1
F32 = jnp.float32
BF16 = jnp.bfloat16
MESH = pl.DeviceIdType.MESH


def dot(left, right):
    return jnp.dot(left, right, preferred_element_type=F32)


def dot_rows(left, right):
    return lax.dot_general(left, right, (((1,), (1,)), ((), ())), preferred_element_type=F32)


def dot_columns(left, right):
    return lax.dot_general(left, right, (((0,), (0,)), ((), ())), preferred_element_type=F32)


def parts_of(values):
    high = values.astype(BF16)
    return high, (values - high.astype(F32)).astype(BF16)


def plan(level):
    start = 0.008 / 1.008 * math.pi / 2.0
    base = math.cos(start) ** 2
    angle = ((level + 1.0) / 1000.0 + 0.008) / 1.008 * (math.pi / 2.0)
    signal = jnp.cos(angle) ** 2 / base
    remain = jnp.sin(angle - start) * jnp.sin(angle + start) / base
    return (signal, remain)


def shifted(tile, step):
    if step == 1:
        return tile
    width = tile.shape[1]
    lane = lax.broadcasted_iota(jnp.int32, tile.shape, 1)
    if step == 0:
        return jnp.where(lane == 0, 0.0, pltpu.roll(tile, 1, 1))
    return jnp.where(lane == width - 1, 0.0, pltpu.roll(tile, width - 1, 1))


def layer_norm_columns(values):
    centre = values - jnp.mean(values, axis=0, keepdims=True)
    return centre * lax.rsqrt(jnp.mean(centre * centre, axis=0, keepdims=True) + 1e-05)


def turned_rows(tile, step):
    return jnp.concatenate([tile[8 - step :], tile[: 8 - step]], axis=0) if step else tile


def compact(blocks):
    row = lax.broadcasted_iota(jnp.int32, (8, blocks[0].shape[1]), 0)
    pieces = []
    lasts = []
    constants = None
    for index, block in enumerate(blocks):
        tiles = [block[8 * i : 8 * i + 8] for i in range(6)]
        pieces += [tiles[0], tiles[2], tiles[4]]
        odd = [jnp.where(row < 4, tiles[i], 0.0) for i in (1, 3, 5)]
        pieces.append(odd[0] + turned_rows(odd[1], 4))
        lasts.append(odd[2])
        constant = turned_rows(jnp.where(row == 4, tiles[3], 0.0), (index + 4) % 8)
        constants = constant if constants is None else constants + constant
    for first in range(0, len(blocks), 2):
        pieces.append(lasts[first] + turned_rows(lasts[first + 1], 4))
    return jnp.concatenate(pieces + [constants], axis=0)


def kernel(
    sizes,
    steps_hbm,
    latents_hbm,
    noise_hbm,
    conv_in_hbm,
    time_hbm,
    spatial_in_hbm,
    spatial_out_hbm,
    temporal_in_hbm,
    temporal_out_hbm,
    conv_out_hbm,
    denoised_ref,
    queue_ref,
    steps_ref,
    latents_ref,
    noise_ref,
    conv_in_ref,
    time_ref,
    spatial_in_ref,
    spatial_out_ref,
    temporal_in_ref,
    temporal_out_ref,
    conv_out_ref,
    conv_in_t,
    score_w,
    mixed_w,
    temporal_in_t,
    temporal_out_t,
    conv_out_t,
    common_w,
    slot_w,
    frame_ref,
    entered_ref,
    patch_ref,
    scaled_ref,
    score_ref,
    weight_ref,
    tkv_ref,
    rows_ref,
    sent_ref,
    beside_ref,
    factor_sent_ref,
    factor_ref,
    own_lean_ref,
    lean_ref,
    zeros_ref,
    calm_ref,
    silent_ref,
    parts_ref,
    own_out_ref,
    next_out_ref,
    own_in_ref,
    load_sem,
    rows_send,
    rows_recv,
    beside_send,
    beside_recv,
    factor_send,
    factor_recv,
    lean_send,
    lean_recv,
    next_send,
    next_recv,
    own_send,
    own_recv,
):
    queue_len, row_len, comm = sizes
    channels = time_ref.shape[0]
    head_dim = channels // HEADS
    width = latents_ref.shape[3]
    pixels = row_len * width
    if comm:
        me_q = lax.axis_index("queue")
        me_r = lax.axis_index("row")
    else:
        me_q = 5
        me_r = 3
    core = lax.rem(me_q, 2)
    sibling = me_q + 1 - 2 * core
    last_frame = queue_len - 1
    side = lax.rem(lax.div(me_q, 2), 2)
    beside = 2 - 4 * side
    three = 6 * core - 3
    reach = me_q + core * (last_frame - 2 * me_q)
    cross_good = me_q + side * (last_frame - 2 * me_q) >= 2

    def row_at(offset):
        return lax.rem(me_r + offset + row_len, row_len)

    ring = row_len // 2
    steps = sorted(
        ((flip, turn) for flip in range(2) for turn in range(ring)),
        key=lambda way: -2 * way[0] - min(way[1], ring - way[1]),
    )

    def row_by(flip, turn):
        here = lax.div(me_r, ring)
        return lax.rem(here + flip, 2) * ring + lax.rem(me_r - here * ring + turn, ring)

    def send(source, target, send_sem, recv_sem, device):
        return pltpu.make_async_remote_copy(
            src_ref=source,
            dst_ref=target,
            send_sem=send_sem,
            recv_sem=recv_sem,
            device_id=device,
            device_id_type=MESH,
        )

    if comm:
        barrier = pltpu.get_barrier_semaphore()

        def greet(q, r):
            pl.semaphore_signal(barrier, inc=1, device_id=(q, r), device_id_type=MESH)

        for flip, turn in steps[:-1]:
            greet(me_q, row_by(flip, turn))
        greet(sibling, me_r)
        for distance in (2, 4):

            @pl.when(me_q + distance <= last_frame)
            def _():
                greet(me_q + distance, me_r)

            @pl.when(me_q - distance >= 0)
            def _():
                greet(me_q - distance, me_r)

    loads = [
        pltpu.make_async_copy(source, target, load_sem.at[index])
        for index, (source, target) in enumerate(
            (
                (latents_hbm, latents_ref),
                (noise_hbm, noise_ref),
                (steps_hbm, steps_ref),
                (time_hbm, time_ref),
                (conv_in_hbm, conv_in_ref),
                (spatial_in_hbm, spatial_in_ref),
                (spatial_out_hbm, spatial_out_ref),
                (temporal_in_hbm, temporal_in_ref),
                (temporal_out_hbm, temporal_out_ref),
                (conv_out_hbm, conv_out_ref),
            )
        )
    ]
    for load in loads:
        load.start()

    loads[0].wait()
    loads[1].wait()
    latents = latents_ref[0, :, 0, :]
    empty = jnp.zeros_like(latents)
    state = jnp.concatenate([latents, empty], axis=0)
    rows_ref[me_r] = jnp.concatenate([latents, noise_ref[0, :, 0, :]], axis=0)

    loads[2].wait()
    level_now = steps_ref[0, 0].astype(F32)
    level_next = steps_ref[0, 1].astype(F32)
    signal_now, rest_now = plan(jnp.full((8, width), level_now, F32))
    signal_next, rest_next = plan(jnp.full((8, width), level_next, F32))
    keep = jnp.sqrt(signal_next) / jnp.sqrt(signal_now)
    push = jnp.sqrt(rest_next) - keep * jnp.sqrt(rest_now)

    half = channels // 2
    column = lax.broadcasted_iota(jnp.int32, (8, channels), 1)
    place = jnp.where(column < half, column, column - half).astype(F32)
    angle = level_now * jnp.exp(place * (-math.log(10000.0) / half))
    embedding = jnp.where(column < half, jnp.cos(angle), jnp.sin(angle)).astype(BF16)
    loads[3].wait()
    projected = dot(embedding, time_ref[...])
    bias = projected[0:1] / (1.0 + jnp.exp(-projected[0:1]))
    bias = bias - jnp.mean(bias, axis=1, keepdims=True)

    loads[4].wait()
    wide = conv_in_ref[...].astype(F32)
    wide = wide - jnp.mean(wide, axis=1, keepdims=True)
    gap = jnp.zeros((4, channels), F32)
    lone = jnp.concatenate([bias, gap[0:3]], axis=0)
    centred = jnp.concatenate(
        [wide[0:12], gap, wide[12:24], lone, wide[24:36], gap], axis=0
    )
    rows = centred.shape[0]
    high, low = parts_of(centred)
    conv_in_t[...] = jnp.concatenate([high, low], axis=0).astype(F32).T.astype(BF16)

    if comm:
        def reaches(space, distance):
            return lax.div(space + queue_len - distance, queue_len)

        greeted = row_len
        for space in (me_q, last_frame - me_q):
            greeted += reaches(space, 2) + reaches(space, 4)
        pl.semaphore_wait(barrier, greeted)

    row_copies = []
    if comm:
        for flip, turn in steps[:-1]:
            copy = send(
                rows_ref.at[me_r],
                rows_ref.at[me_r],
                rows_send.at[ring * flip + turn],
                rows_recv.at[ring * flip + turn],
                (me_q, row_by(flip, turn)),
            )
            copy.start()
            row_copies.append(copy)

    loads[5].wait()
    seen = dot(high, spatial_in_ref[...]) + dot(low, spatial_in_ref[...])
    head_of = lax.broadcasted_iota(jnp.int32, (rows, channels), 1) // head_dim

    def by_head(values, slots=False):
        pieces = []
        for head in range(HEADS):
            own = jnp.where(head_of == head, values, 0.0)
            pieces += [own, own, jnp.zeros((128 - 2 * rows, channels), F32)] if slots else [own]
        return jnp.concatenate(pieces, axis=0)

    query_high, query_low = parts_of(seen[:, :channels])
    key_high, key_low = parts_of(by_head(seen[:, channels : 2 * channels], True))
    product = (
        dot_rows(query_high, key_high)
        + dot_rows(query_low, key_high)
        + dot_rows(query_high, key_low)
    ) * (1.0 / math.sqrt(head_dim))
    high, low = parts_of(product)
    score_w[0:rows] = high
    score_w[rows : 2 * rows] = high
    score_w[2 * rows : 128] = jnp.zeros((128 - 2 * rows, HEADS * 128), BF16)
    score_w[128 : 128 + rows] = low
    loads[6].wait()
    turned = spatial_out_ref[...].T
    values = by_head(seen[:, 2 * channels :])
    value_high, value_low = parts_of(jnp.concatenate([values] * 3, axis=0))
    product = dot_rows(turned, value_high) + dot_rows(turned, value_low)
    product = product - jnp.mean(product, axis=0, keepdims=True)
    high, low = parts_of(product)
    third = lax.broadcasted_iota(jnp.int32, product.shape, 1) // (HEADS * rows)
    mixed_w[...] = jnp.where(third < 2, high.astype(F32), low.astype(F32)).astype(BF16)

    loads[7].wait()
    value_high, value_low = parts_of(values)
    product = dot(value_high, spatial_out_ref[...]) + dot(value_low, spatial_out_ref[...])
    wide = compact([centred] + [product[rows * h : rows * (h + 1)] for h in range(HEADS)])
    wide = wide - jnp.mean(wide, axis=1, keepdims=True)
    high, low = parts_of(wide)
    product = dot(high, temporal_in_ref[:, channels:]) + dot(low, temporal_in_ref[:, channels:])
    sides = lax.broadcasted_iota(jnp.int32, product.shape, 0) < 216
    common_w[...] = jnp.where(sides, product, 0.0).T.astype(BF16)
    own_lean_ref[...] = jnp.where(sides, 0.0, product)[208:224].astype(BF16)

    frames = (
        me_q - beside,
        me_q + beside,
        me_q - 4,
        me_q + 4,
        sibling,
        sibling + beside,
        me_q + three,
        sibling - beside,
    )
    unsent = list(row_copies)
    guarded_unsent = []

    def scatter(source, targets, send_sems, recv_sems):
        for slot, target, good in (
            (0, me_q - beside, cross_good),
            (1, me_q + beside, True),
            (3, me_q - 4, me_q >= 4),
            (2, me_q + 4, me_q + 4 <= last_frame),
            (4, sibling, True),
        ):
            copy = send(
                source, targets.at[slot], send_sems.at[slot], recv_sems.at[slot], (target, me_r)
            )
            if good is True:
                copy.start()
                unsent.append(copy)
            else:
                pl.when(good)(copy.start)
                guarded_unsent.append((good, copy))

    def fill(zeros, targets, recv_sems):
        for slot, good in (
            (0, cross_good),
            (2, me_q >= 4),
            (3, me_q + 4 <= last_frame),
        ):
            copy = pltpu.make_async_copy(zeros, targets.at[slot], recv_sems.at[slot])
            pl.when(jnp.logical_not(good))(copy.start)

    def arrived(slot, targets, send_sems, recv_sems):
        copy = send(
            targets.at[slot], targets.at[slot], send_sems.at[slot], recv_sems.at[slot], (sibling, me_r)
        )
        copy.wait_recv()

    def relay(slot, target, targets, send_sems, recv_sems):
        copy = send(
            targets.at[slot],
            targets.at[target],
            send_sems.at[target],
            recv_sems.at[target],
            (sibling, me_r),
        )
        copy.start()
        unsent.append(copy)

    def settle():
        for copy in unsent:
            copy.wait_send()
        for good, copy in guarded_unsent:
            pl.when(good)(copy.wait_send)
        unsent.clear()
        guarded_unsent.clear()

    if comm:
        leans = (lean_ref, lean_send, lean_recv)
        zeros_ref[...] = jnp.zeros(zeros_ref.shape, BF16)
        calm_ref[...] = jnp.zeros(calm_ref.shape, F32)
        silent_ref[...] = jnp.zeros(silent_ref.shape, BF16)
        fill(silent_ref, lean_ref, lean_recv)
        for step in range(STEPS):
            fill(zeros_ref, beside_ref.at[step], beside_recv.at[step])
            fill(calm_ref, factor_ref.at[step], factor_recv.at[step])
        scatter(own_lean_ref, *leans)

    temporal_in_t[...] = temporal_in_ref[...].T
    loads[8].wait()
    temporal_out_t[...] = temporal_out_ref[...].T
    loads[9].wait()
    turned = conv_out_ref[...].astype(F32)
    pieces = []
    for col_step in range(3):
        for row_step in range(3):
            base = 4 * (3 * row_step + col_step)
            pieces.append(turned[base : base + 4])
            pieces.append(gap)
    pieces.append(jnp.zeros((8, channels), F32))
    conv_out_t[...] = jnp.concatenate(pieces, axis=0).astype(BF16)
    scaled_ref[2 * rows : 2 * rows + 16, :] = jnp.ones((16, pixels), BF16)
    scaled_ref[2 * rows + 16 : 128, :] = jnp.zeros((128 - 2 * rows - 16, pixels), BF16)
    scaled_ref[128 + rows :, :] = jnp.zeros((128 - rows, pixels), BF16)

    for copy in row_copies:
        copy.wait_recv()

    own_columns = pl.ds(pl.multiple_of(me_r * width, width), width)
    sublane = lax.broadcasted_iota(jnp.int32, (8, width), 0)
    upper = sublane < 4
    constant = jnp.where(sublane == 4, 1.0, 0.0)
    own_copies = []
    next_sent = []
    middles = []
    images = []
    for y in range(row_len):
        images.append(jnp.where(upper, rows_ref[y], 0.0))
        entered_ref[y] = jnp.where(upper, pltpu.roll(rows_ref[y], 4, 0), 0.0)

    for step in range(STEPS):
        tiles = []
        for y in range(row_len):
            tile = images[y]
            tiles.append(
                jnp.concatenate(
                    [shifted(tile, 0) + pltpu.roll(tile, 4, 0), shifted(tile, 2) + constant],
                    axis=0,
                ).astype(BF16)
            )
        nothing = jnp.zeros_like(tiles[0])
        for y in range(row_len):
            for a in range(3):
                other = y + a - 1
                patch_ref[16 * a : 16 * a + 16, y * width : (y + 1) * width] = (
                    tiles[other] if 0 <= other < row_len else nothing
                )

        chunk = 2 * width
        for lower in range(0, pixels, chunk):
            span = slice(lower, lower + chunk)
            patch = patch_ref[:, span]
            hidden = dot(conv_in_t[...], jnp.concatenate([patch, patch], axis=0))
            factor = lax.rsqrt(jnp.mean(hidden * hidden, axis=0, keepdims=True) + 1e-05)
            high, low = parts_of(patch.astype(F32) * factor)
            scaled_ref[0:rows, span] = high
            scaled_ref[rows : 2 * rows, span] = low
            scaled_ref[128 : 128 + rows, span] = high

        patch = patch_ref[:, own_columns]
        hidden = dot(conv_in_t[...], jnp.concatenate([patch, patch], axis=0))
        queries = dot_columns(scaled_ref[0 : 128 + rows, own_columns], score_w[...])
        high, low = parts_of(queries)
        lefts = [
            jnp.concatenate(
                [high[:, 128 * head : 128 * head + 128], low[:, 128 * head : 128 * head + 128]],
                axis=1,
            )
            for head in range(HEADS)
        ]
        groups = ((0, 2), (2, 4), (4, 5))
        for first, after in groups:
            score_ref[first * width : after * width, :] = dot(
                jnp.concatenate(lefts[first:after], axis=0), scaled_ref[...]
            )
        summed = []
        for first, after in groups:
            for lower in range(first * width, after * width, 32):
                block = score_ref[lower : lower + 32, :]
                peak = jnp.max(block, axis=1, keepdims=True)
                weight_ref[lower : lower + 32, :] = jnp.exp(block - peak).astype(BF16)
            summed.append(
                dot_rows(
                    scaled_ref[rows : 128 + rows, :], weight_ref[first * width : after * width, :]
                )
            )
        summed = jnp.concatenate(summed, axis=1)
        mixed = (summed[0:rows] + summed[128 - rows : 128]) / summed[rows : rows + 1]
        mixed = [mixed[:, width * head : width * (head + 1)] for head in range(HEADS)]
        sent_ref[step] = compact([patch.astype(F32)] + mixed).astype(BF16)
        if comm:
            before = (list(unsent), list(guarded_unsent))
            unsent.clear()
            guarded_unsent.clear()
            groups = [
                tuple(ref.at[step] for ref in (beside_ref, beside_send, beside_recv)),
                tuple(ref.at[step] for ref in (factor_ref, factor_send, factor_recv)),
            ]
            scatter(sent_ref.at[step], *groups[0])
        high, low = parts_of(jnp.concatenate(mixed, axis=0))
        hidden = hidden + dot(mixed_w[...], jnp.concatenate([high, low, high], axis=0))
        factor = lax.rsqrt(jnp.mean(hidden * hidden, axis=0, keepdims=True) + 1e-05)
        factor_sent_ref[step] = jnp.broadcast_to(factor, (8, width))
        if comm:
            scatter(factor_sent_ref.at[step], *groups[1])
        normed = (hidden * factor).astype(BF16)

        projected = dot(temporal_in_t[...], normed).astype(BF16).astype(F32)
        tqueries = projected[:channels] * (1.0 / math.sqrt(head_dim))
        tkv_ref[2 * HALF] = projected[2 * channels :]
        scores = [None] * SPAN

        def score_of(keys):
            return jnp.concatenate(
                [
                    jnp.sum(
                        tqueries[h * head_dim : (h + 1) * head_dim]
                        * keys[h * head_dim : (h + 1) * head_dim],
                        axis=0,
                        keepdims=True,
                    )
                    for h in range(HEADS)
                ],
                axis=0,
            )

        def take(slots):
            for slot in slots:
                part = dot(slot_w[slot], beside_ref[step, slot])
                part = (part * factor_ref[step, slot, 0:1, :]).astype(BF16).astype(F32)
                good = jnp.logical_and(frames[slot] >= 0, frames[slot] <= last_frame)
                scores[slot] = jnp.where(good, score_of(part[:channels]), -jnp.inf)
                tkv_ref[slot] = part[channels:]

        scores[2 * HALF] = score_of(projected[channels : 2 * channels])

        def receive(*slots, groups=groups if comm else ()):
            for slot in slots:
                for group in groups:
                    arrived(slot, *group)

        def pass_on(slot, target, groups=groups[::-1] if comm else ()):
            for group in groups:
                relay(slot, target, *group)

        if step == 0:
            only = [leans] if comm else ()
            receive(0, 1, 2, 3, 4, groups=only)
            pass_on(3 - core, 6, groups=only)
            pass_on(1, 5, groups=only)
            pass_on(0, 7, groups=only)
            shape = (16, common_w.shape[1])
            place = lax.broadcasted_iota(jnp.int32, shape, 1)
            row = lax.broadcasted_iota(jnp.int32, shape, 0)
            spread = jnp.where(place == row + 208, 1.0, 0.0).astype(BF16)

            def weave(slot):
                slot_w[slot] = (
                    common_w[...].astype(F32) + dot_columns(lean_ref[slot], spread)
                ).astype(BF16)

            for slot in (4, 2, 3, 0, 1):
                weave(slot)
            receive(6, 5, 7, groups=only)
            for slot in (6, 5, 7):
                weave(slot)

        def weigh(slots, peak):
            weights = [jnp.exp(scores[slot] - peak) for slot in slots]
            total = functools.reduce(jnp.add, weights)
            rounded = [weight.astype(BF16).astype(F32) for weight in weights]
            mixed = []
            for head in range(HEADS):
                blended = None
                for slot, weight in zip(slots, rounded):
                    term = (
                        weight[head : head + 1]
                        * tkv_ref[slot, head * head_dim : (head + 1) * head_dim, :]
                    )
                    blended = term if blended is None else blended + term
                mixed.append(blended)
            return total, mixed

        if comm:
            after = (list(unsent), list(guarded_unsent))
            unsent[:], guarded_unsent[:] = before
            settle()
            unsent[:], guarded_unsent[:] = after
        receive(4)
        take([4])
        receive(2, 3)
        pass_on(3 - core, 6)
        take([2, 3])
        receive(0)
        pass_on(0, 7)
        receive(1)
        pass_on(1, 5)
        take([0, 1])
        receive(6)
        take([6])
        receive(5)
        take([5])
        early = [0, 1, 2, 3, 4, 5, 6, 8]
        early_peak = functools.reduce(jnp.maximum, [scores[slot] for slot in early])
        early_total, early_mixed = weigh(early, early_peak)
        receive(7)
        take([7])
        peak = jnp.maximum(early_peak, scores[7])
        late_total, late_mixed = weigh([7], peak)
        shrink = jnp.exp(early_peak - peak)
        total = early_total * shrink + late_total
        mixed = [
            (early_mixed[head] * shrink[head : head + 1] + late_mixed[head])
            / total[head : head + 1]
            for head in range(HEADS)
        ]
        mixed = jnp.concatenate(mixed, axis=0).astype(BF16)
        hidden = hidden + dot(temporal_out_t[...], mixed)
        normed = layer_norm_columns(hidden).astype(BF16)

        taps = dot(conv_out_t[...], normed)
        added = shifted(taps[0:24], 0) + taps[24:48] + shifted(taps[48:72], 2)
        below = push * added[0:8]
        middle = push * added[8:16] + keep * state
        above = push * added[16:24]
        middles.append(middle)
        own_out_ref[step, 0] = below
        own_out_ref[step, 1] = above
        next_out_ref[step, 0:8] = middle
        next_out_ref[step, 8:16] = below + pltpu.roll(above, 4, 0)

        last = step == STEPS - 1
        next_copies = []
        if comm:
            if last:
                ways = [(index, row_at(offset)) for index, offset in enumerate((1, -1, 0))]
            else:
                ways = [(ring * flip + turn, row_by(flip, turn)) for flip, turn in steps]
            for index, target in ways:
                copy = send(
                    next_out_ref.at[step],
                    parts_ref.at[step, me_r],
                    next_send.at[step, index],
                    next_recv.at[step, index],
                    (me_q - 1, target),
                )
                next_copies.append(copy)

            @pl.when(me_q > 0)
            def _():
                for copy in next_copies:
                    copy.start()

            for slot, offset in enumerate((1, -1)):
                copy = send(
                    own_out_ref.at[step, slot],
                    own_in_ref.at[step, slot],
                    own_send.at[step, slot],
                    own_recv.at[step, slot],
                    (me_q, row_at(offset)),
                )
                copy.start()
                own_copies.append(copy)
            if last:
                settle()

            @pl.when(me_q < last_frame)
            def _():
                for copy in next_copies:
                    copy.wait_recv()

            next_sent.append(next_copies)
        entering = me_q == last_frame
        if not last:
            images = []
            for y in range(row_len):
                total = parts_ref[step, y, 0:8]
                if y > 0:
                    total = total + parts_ref[step, y - 1, 8:16]
                if y < row_len - 1:
                    total = total + pltpu.roll(parts_ref[step, y + 1, 8:16], 4, 0)
                total = jnp.where(entering, entered_ref[y], jnp.where(upper, total, 0.0))
                images.append(total)
                frame_ref[y] = total
            state = frame_ref[me_r]
        else:
            total = parts_ref[step, me_r, 0:8]
            total = total + jnp.where(me_r == 0, 0.0, parts_ref[step, row_at(-1), 8:16])
            total = total + jnp.where(
                me_r == row_len - 1, 0.0, pltpu.roll(parts_ref[step, row_at(1), 8:16], 4, 0)
            )
            queue_ref[0, :, 0, :] = jnp.where(entering, noise_ref[step, :, 0, :], total[0:4])

    for copy in own_copies:
        copy.wait()
    for step in range(STEPS):
        total = middles[step]
        total = total + jnp.where(me_r == 0, 0.0, own_in_ref[step, 0])
        total = total + jnp.where(me_r == row_len - 1, 0.0, own_in_ref[step, 1])
        denoised_ref[step, 0, :, 0, :] = total[0:4]
    if comm:
        settle()

        @pl.when(me_q > 0)
        def _():
            for next_copies in next_sent:
                for copy in next_copies:
                    copy.wait_send()


def on_device(
    latents,
    fresh_noise,
    timesteps,
    conv_in_w,
    time_w,
    spatial_in,
    spatial_out,
    temporal_in,
    temporal_out,
    conv_out_w,
    *,
    sizes,
):
    queue_len, row_len, comm = sizes
    channels = conv_in_w.shape[1]
    width = latents.shape[3]
    pixels = row_len * width
    vmem = pl.BlockSpec(memory_space=pltpu.VMEM)
    hbm = pl.BlockSpec(memory_space=pl.ANY)
    dma = pltpu.SemaphoreType.DMA
    weights = (conv_in_w, time_w, spatial_in, spatial_out, temporal_in, temporal_out, conv_out_w.T)
    arguments = (timesteps, latents, fresh_noise) + weights
    return pl.pallas_call(
        functools.partial(kernel, sizes),
        out_shape=(
            jax.ShapeDtypeStruct((STEPS,) + latents.shape, F32),
            jax.ShapeDtypeStruct(latents.shape, F32),
        ),
        in_specs=[hbm] * len(arguments),
        out_specs=(vmem, vmem),
        scratch_shapes=[pltpu.SMEM(timesteps.shape, timesteps.dtype)]
        + [pltpu.VMEM(array.shape, array.dtype) for array in arguments[1:]]
        + [
            pltpu.VMEM((channels, 96), BF16),
            pltpu.VMEM((176, HEADS * 128), BF16),
            pltpu.VMEM((channels, 3 * HEADS * 48), BF16),
            pltpu.VMEM((3 * channels, channels), BF16),
            pltpu.VMEM((channels, channels), BF16),
            pltpu.VMEM((80, channels), BF16),
            pltpu.VMEM((2 * channels, 224), BF16),
            pltpu.VMEM((2 * HALF, 2 * channels, 224), BF16),
            pltpu.VMEM((row_len, 8, width), F32),
            pltpu.VMEM((row_len, 8, width), F32),
            pltpu.VMEM((48, pixels), BF16),
            pltpu.VMEM((256, pixels), BF16),
            pltpu.VMEM((HEADS * width, pixels), F32),
            pltpu.VMEM((HEADS * width, pixels), BF16),
            pltpu.VMEM((SPAN, channels, width), F32),
            pltpu.VMEM((row_len, 8, width), F32),
            pltpu.VMEM((STEPS, 224, width), BF16),
            pltpu.VMEM((STEPS, 2 * HALF, 224, width), BF16),
            pltpu.VMEM((STEPS, 8, width), F32),
            pltpu.VMEM((STEPS, 2 * HALF, 8, width), F32),
            pltpu.VMEM((16, 2 * channels), BF16),
            pltpu.VMEM((2 * HALF, 16, 2 * channels), BF16),
            pltpu.VMEM((224, width), BF16),
            pltpu.VMEM((8, width), F32),
            pltpu.VMEM((16, 2 * channels), BF16),
            pltpu.VMEM((STEPS, row_len, 16, width), F32),
            pltpu.VMEM((STEPS, 2, 8, width), F32),
            pltpu.VMEM((STEPS, 16, width), F32),
            pltpu.VMEM((STEPS, 2, 8, width), F32),
            dma((len(arguments),)),
            dma((row_len,)),
            dma((row_len,)),
            dma((STEPS, 2 * HALF)),
            dma((STEPS, 2 * HALF)),
            dma((STEPS, 2 * HALF)),
            dma((STEPS, 2 * HALF)),
            dma((2 * HALF,)),
            dma((2 * HALF,)),
            dma((STEPS, row_len)),
            dma((STEPS, row_len)),
            dma((STEPS, 2)),
            dma((STEPS, 2)),
        ],
        compiler_params=pltpu.CompilerParams(
            collective_id=0 if comm else None,
            has_side_effects=True,
            vmem_limit_bytes=40 * 1024 * 1024,
        ),
        name="denoise",
    )(*(pltpu.with_memory_space_constraint(array, pltpu.HBM) for array in arguments))


def solution(mesh):
    sizes = (mesh.shape["queue"], mesh.shape["row"], True)
    return jax.shard_map(
        functools.partial(on_device, sizes=sizes),
        mesh=mesh,
        in_specs=(
            P("queue", None, "row", None),
            P(None, None, "row", None),
            P("queue", None),
            P(),
            P(),
            P(),
            P(),
            P(),
            P(),
            P(),
        ),
        out_specs=(P(None, "queue", None, "row", None), P("queue", None, "row", None)),
        check_vma=False,
    )
```

```python
import functools
import math

import jax
import jax.numpy as jnp
from jax import lax
from jax.experimental import pallas as pl
from jax.experimental.pallas import tpu as pltpu
from jax.sharding import PartitionSpec as P

HEADS = 5
HALF = 4
STEPS = 2
SPAN = 2 * HALF + 1
F32 = jnp.float32
BF16 = jnp.bfloat16
MESH = pl.DeviceIdType.MESH


def dot(left, right):
    return jnp.dot(left, right, preferred_element_type=F32)


def dot_rows(left, right):
    return lax.dot_general(left, right, (((1,), (1,)), ((), ())), preferred_element_type=F32)


def dot_columns(left, right):
    return lax.dot_general(left, right, (((0,), (0,)), ((), ())), preferred_element_type=F32)


def parts_of(values):
    high = values.astype(BF16)
    return high, (values - high.astype(F32)).astype(BF16)


def plan(level):
    start = 0.008 / 1.008 * math.pi / 2.0
    base = math.cos(start) ** 2
    angle = ((level + 1.0) / 1000.0 + 0.008) / 1.008 * (math.pi / 2.0)
    signal = jnp.cos(angle) ** 2 / base
    remain = jnp.sin(angle - start) * jnp.sin(angle + start) / base
    return (signal, remain)


def shifted(tile, step):
    if step == 1:
        return tile
    width = tile.shape[1]
    lane = lax.broadcasted_iota(jnp.int32, tile.shape, 1)
    if step == 0:
        return jnp.where(lane == 0, 0.0, pltpu.roll(tile, 1, 1))
    return jnp.where(lane == width - 1, 0.0, pltpu.roll(tile, width - 1, 1))


def layer_norm_columns(values):
    centre = values - jnp.mean(values, axis=0, keepdims=True)
    return centre * lax.rsqrt(jnp.mean(centre * centre, axis=0, keepdims=True) + 1e-05)


def turned_rows(tile, step):
    return jnp.concatenate([tile[8 - step :], tile[: 8 - step]], axis=0) if step else tile


def compact(blocks):
    row = lax.broadcasted_iota(jnp.int32, (8, blocks[0].shape[1]), 0)
    pieces = []
    lasts = []
    constants = None
    for index, block in enumerate(blocks):
        tiles = [block[8 * i : 8 * i + 8] for i in range(6)]
        pieces += [tiles[0], tiles[2], tiles[4]]
        odd = [jnp.where(row < 4, tiles[i], 0.0) for i in (1, 3, 5)]
        pieces.append(odd[0] + turned_rows(odd[1], 4))
        lasts.append(odd[2])
        constant = turned_rows(jnp.where(row == 4, tiles[3], 0.0), (index + 4) % 8)
        constants = constant if constants is None else constants + constant
    for first in range(0, len(blocks), 2):
        pieces.append(lasts[first] + turned_rows(lasts[first + 1], 4))
    return jnp.concatenate(pieces + [constants], axis=0)


def kernel(
    sizes,
    steps_hbm,
    latents_hbm,
    noise_hbm,
    conv_in_hbm,
    time_hbm,
    spatial_in_hbm,
    spatial_out_hbm,
    temporal_in_hbm,
    temporal_out_hbm,
    conv_out_hbm,
    denoised_ref,
    queue_ref,
    steps_ref,
    latents_ref,
    noise_ref,
    conv_in_ref,
    time_ref,
    spatial_in_ref,
    spatial_out_ref,
    temporal_in_ref,
    temporal_out_ref,
    conv_out_ref,
    conv_in_t,
    score_w,
    mixed_w,
    temporal_in_t,
    temporal_out_t,
    conv_out_t,
    common_w,
    slot_w,
    frame_ref,
    entered_ref,
    patch_ref,
    scaled_ref,
    score_ref,
    weight_ref,
    tkv_ref,
    rows_ref,
    sent_ref,
    beside_ref,
    factor_sent_ref,
    factor_ref,
    own_lean_ref,
    lean_ref,
    zeros_ref,
    calm_ref,
    silent_ref,
    parts_ref,
    own_out_ref,
    next_out_ref,
    own_in_ref,
    load_sem,
    rows_send,
    rows_recv,
    beside_send,
    beside_recv,
    factor_send,
    factor_recv,
    lean_send,
    lean_recv,
    next_send,
    next_recv,
    own_send,
    own_recv,
):
    queue_len, row_len, comm = sizes
    channels = time_ref.shape[0]
    head_dim = channels // HEADS
    width = latents_ref.shape[3]
    pixels = row_len * width
    if comm:
        me_q = lax.axis_index("queue")
        me_r = lax.axis_index("row")
    else:
        me_q = 5
        me_r = 3
    core = lax.rem(me_q, 2)
    sibling = me_q + 1 - 2 * core
    last_frame = queue_len - 1
    side = lax.rem(lax.div(me_q, 2), 2)
    beside = 2 - 4 * side
    three = 6 * core - 3
    reach = me_q + core * (last_frame - 2 * me_q)
    cross_good = me_q + side * (last_frame - 2 * me_q) >= 2

    def row_at(offset):
        return lax.rem(me_r + offset + row_len, row_len)

    ring = row_len // 2
    steps = sorted(
        ((flip, turn) for flip in range(2) for turn in range(ring)),
        key=lambda way: -2 * way[0] - min(way[1], ring - way[1]),
    )

    def row_by(flip, turn):
        here = lax.div(me_r, ring)
        return lax.rem(here + flip, 2) * ring + lax.rem(me_r - here * ring + turn, ring)

    def send(source, target, send_sem, recv_sem, device):
        return pltpu.make_async_remote_copy(
            src_ref=source,
            dst_ref=target,
            send_sem=send_sem,
            recv_sem=recv_sem,
            device_id=device,
            device_id_type=MESH,
        )

    if comm:
        barrier = pltpu.get_barrier_semaphore()

        def greet(q, r):
            pl.semaphore_signal(barrier, inc=1, device_id=(q, r), device_id_type=MESH)

        for flip, turn in steps[:-1]:
            greet(me_q, row_by(flip, turn))
        greet(sibling, me_r)
        for distance in (2, 4):

            @pl.when(me_q + distance <= last_frame)
            def _():
                greet(me_q + distance, me_r)

            @pl.when(me_q - distance >= 0)
            def _():
                greet(me_q - distance, me_r)

    loads = [
        pltpu.make_async_copy(source, target, load_sem.at[index])
        for index, (source, target) in enumerate(
            (
                (latents_hbm, latents_ref),
                (noise_hbm, noise_ref),
                (steps_hbm, steps_ref),
                (time_hbm, time_ref),
                (conv_in_hbm, conv_in_ref),
                (spatial_in_hbm, spatial_in_ref),
                (spatial_out_hbm, spatial_out_ref),
                (temporal_in_hbm, temporal_in_ref),
                (temporal_out_hbm, temporal_out_ref),
                (conv_out_hbm, conv_out_ref),
            )
        )
    ]
    for load in loads:
        load.start()

    loads[0].wait()
    loads[1].wait()
    latents = latents_ref[0, :, 0, :]
    empty = jnp.zeros_like(latents)
    state = jnp.concatenate([latents, empty], axis=0)
    rows_ref[me_r] = jnp.concatenate([latents, noise_ref[0, :, 0, :]], axis=0)

    loads[2].wait()
    level_now = steps_ref[0, 0].astype(F32)
    level_next = steps_ref[0, 1].astype(F32)
    signal_now, rest_now = plan(jnp.full((8, width), level_now, F32))
    signal_next, rest_next = plan(jnp.full((8, width), level_next, F32))
    keep = jnp.sqrt(signal_next) / jnp.sqrt(signal_now)
    push = jnp.sqrt(rest_next) - keep * jnp.sqrt(rest_now)

    half = channels // 2
    column = lax.broadcasted_iota(jnp.int32, (8, channels), 1)
    place = jnp.where(column < half, column, column - half).astype(F32)
    angle = level_now * jnp.exp(place * (-math.log(10000.0) / half))
    embedding = jnp.where(column < half, jnp.cos(angle), jnp.sin(angle)).astype(BF16)
    loads[3].wait()
    projected = dot(embedding, time_ref[...])
    bias = projected[0:1] / (1.0 + jnp.exp(-projected[0:1]))
    bias = bias - jnp.mean(bias, axis=1, keepdims=True)

    loads[4].wait()
    wide = conv_in_ref[...].astype(F32)
    wide = wide - jnp.mean(wide, axis=1, keepdims=True)
    gap = jnp.zeros((4, channels), F32)
    lone = jnp.concatenate([bias, gap[0:3]], axis=0)
    centred = jnp.concatenate(
        [wide[0:12], gap, wide[12:24], lone, wide[24:36], gap], axis=0
    )
    rows = centred.shape[0]
    high, low = parts_of(centred)
    conv_in_t[...] = jnp.concatenate([high, low], axis=0).astype(F32).T.astype(BF16)

    if comm:
        def reaches(space, distance):
            return lax.div(space + queue_len - distance, queue_len)

        greeted = row_len
        for space in (me_q, last_frame - me_q):
            greeted += reaches(space, 2) + reaches(space, 4)
        pl.semaphore_wait(barrier, greeted)

    row_copies = []
    if comm:
        for flip, turn in steps[:-1]:
            copy = send(
                rows_ref.at[me_r],
                rows_ref.at[me_r],
                rows_send.at[ring * flip + turn],
                rows_recv.at[ring * flip + turn],
                (me_q, row_by(flip, turn)),
            )
            copy.start()
            row_copies.append(copy)

    loads[5].wait()
    seen = dot(high, spatial_in_ref[...]) + dot(low, spatial_in_ref[...])
    head_of = lax.broadcasted_iota(jnp.int32, (rows, channels), 1) // head_dim

    def by_head(values, slots=False):
        pieces = []
        for head in range(HEADS):
            own = jnp.where(head_of == head, values, 0.0)
            pieces += [own, own, jnp.zeros((128 - 2 * rows, channels), F32)] if slots else [own]
        return jnp.concatenate(pieces, axis=0)

    query_high, query_low = parts_of(seen[:, :channels])
    key_high, key_low = parts_of(by_head(seen[:, channels : 2 * channels], True))
    product = (
        dot_rows(query_high, key_high)
        + dot_rows(query_low, key_high)
        + dot_rows(query_high, key_low)
    ) * (1.0 / math.sqrt(head_dim))
    high, low = parts_of(product)
    score_w[0:rows] = high
    score_w[rows : 2 * rows] = high
    score_w[2 * rows : 128] = jnp.zeros((128 - 2 * rows, HEADS * 128), BF16)
    score_w[128 : 128 + rows] = low
    loads[6].wait()
    turned = spatial_out_ref[...].T
    values = by_head(seen[:, 2 * channels :])
    value_high, value_low = parts_of(jnp.concatenate([values] * 3, axis=0))
    product = dot_rows(turned, value_high) + dot_rows(turned, value_low)
    product = product - jnp.mean(product, axis=0, keepdims=True)
    high, low = parts_of(product)
    third = lax.broadcasted_iota(jnp.int32, product.shape, 1) // (HEADS * rows)
    mixed_w[...] = jnp.where(third < 2, high.astype(F32), low.astype(F32)).astype(BF16)

    loads[7].wait()
    value_high, value_low = parts_of(values)
    product = dot(value_high, spatial_out_ref[...]) + dot(value_low, spatial_out_ref[...])
    wide = compact([centred] + [product[rows * h : rows * (h + 1)] for h in range(HEADS)])
    wide = wide - jnp.mean(wide, axis=1, keepdims=True)
    high, low = parts_of(wide)
    product = dot(high, temporal_in_ref[:, channels:]) + dot(low, temporal_in_ref[:, channels:])
    sides = lax.broadcasted_iota(jnp.int32, product.shape, 0) < 216
    common_w[...] = jnp.where(sides, product, 0.0).T.astype(BF16)
    own_lean_ref[...] = jnp.where(sides, 0.0, product)[208:224].astype(BF16)

    frames = (
        me_q - beside,
        me_q + beside,
        me_q - 4,
        me_q + 4,
        sibling,
        sibling + beside,
        me_q + three,
        sibling - beside,
    )
    unsent = list(row_copies)
    guarded_unsent = []

    def scatter(source, targets, send_sems, recv_sems):
        for slot, target, good in (
            (0, me_q - beside, cross_good),
            (1, me_q + beside, True),
            (3, me_q - 4, me_q >= 4),
            (2, me_q + 4, me_q + 4 <= last_frame),
            (4, sibling, True),
        ):
            copy = send(
                source, targets.at[slot], send_sems.at[slot], recv_sems.at[slot], (target, me_r)
            )
            if good is True:
                copy.start()
                unsent.append(copy)
            else:
                pl.when(good)(copy.start)
                guarded_unsent.append((good, copy))

    def fill(zeros, targets, recv_sems):
        for slot, good in (
            (0, cross_good),
            (2, me_q >= 4),
            (3, me_q + 4 <= last_frame),
        ):
            copy = pltpu.make_async_copy(zeros, targets.at[slot], recv_sems.at[slot])
            pl.when(jnp.logical_not(good))(copy.start)

    def arrived(slot, targets, send_sems, recv_sems):
        copy = send(
            targets.at[slot], targets.at[slot], send_sems.at[slot], recv_sems.at[slot], (sibling, me_r)
        )
        copy.wait_recv()

    def relay(slot, target, targets, send_sems, recv_sems):
        copy = send(
            targets.at[slot],
            targets.at[target],
            send_sems.at[target],
            recv_sems.at[target],
            (sibling, me_r),
        )
        copy.start()
        unsent.append(copy)

    def settle():
        for copy in unsent:
            copy.wait_send()
        for good, copy in guarded_unsent:
            pl.when(good)(copy.wait_send)
        unsent.clear()
        guarded_unsent.clear()

    if comm:
        leans = (lean_ref, lean_send, lean_recv)
        zeros_ref[...] = jnp.zeros(zeros_ref.shape, BF16)
        calm_ref[...] = jnp.zeros(calm_ref.shape, F32)
        silent_ref[...] = jnp.zeros(silent_ref.shape, BF16)
        fill(silent_ref, lean_ref, lean_recv)
        for step in range(STEPS):
            fill(zeros_ref, beside_ref.at[step], beside_recv.at[step])
            fill(calm_ref, factor_ref.at[step], factor_recv.at[step])
        scatter(own_lean_ref, *leans)

    temporal_in_t[...] = temporal_in_ref[...].T
    loads[8].wait()
    temporal_out_t[...] = temporal_out_ref[...].T
    loads[9].wait()
    turned = conv_out_ref[...].astype(F32)
    pieces = []
    for col_step in range(3):
        for row_step in range(3):
            base = 4 * (3 * row_step + col_step)
            pieces.append(turned[base : base + 4])
            pieces.append(gap)
    pieces.append(jnp.zeros((8, channels), F32))
    conv_out_t[...] = jnp.concatenate(pieces, axis=0).astype(BF16)
    scaled_ref[2 * rows : 2 * rows + 16, :] = jnp.ones((16, pixels), BF16)
    scaled_ref[2 * rows + 16 : 128, :] = jnp.zeros((128 - 2 * rows - 16, pixels), BF16)
    scaled_ref[128 + rows :, :] = jnp.zeros((128 - rows, pixels), BF16)

    for copy in row_copies:
        copy.wait_recv()

    own_columns = pl.ds(pl.multiple_of(me_r * width, width), width)
    sublane = lax.broadcasted_iota(jnp.int32, (8, width), 0)
    upper = sublane < 4
    constant = jnp.where(sublane == 4, 1.0, 0.0)
    own_copies = []
    next_sent = []
    middles = []
    images = []
    for y in range(row_len):
        images.append(jnp.where(upper, rows_ref[y], 0.0))
        entered_ref[y] = jnp.where(upper, pltpu.roll(rows_ref[y], 4, 0), 0.0)

    for step in range(STEPS):
        tiles = []
        for y in range(row_len):
            tile = images[y]
            tiles.append(
                jnp.concatenate(
                    [shifted(tile, 0) + pltpu.roll(tile, 4, 0), shifted(tile, 2) + constant],
                    axis=0,
                ).astype(BF16)
            )
        nothing = jnp.zeros_like(tiles[0])
        for y in range(row_len):
            for a in range(3):
                other = y + a - 1
                patch_ref[16 * a : 16 * a + 16, y * width : (y + 1) * width] = (
                    tiles[other] if 0 <= other < row_len else nothing
                )

        chunk = 2 * width
        for lower in range(0, pixels, chunk):
            span = slice(lower, lower + chunk)
            patch = patch_ref[:, span]
            hidden = dot(conv_in_t[...], jnp.concatenate([patch, patch], axis=0))
            factor = lax.rsqrt(jnp.mean(hidden * hidden, axis=0, keepdims=True) + 1e-05)
            high, low = parts_of(patch.astype(F32) * factor)
            scaled_ref[0:rows, span] = high
            scaled_ref[rows : 2 * rows, span] = low
            scaled_ref[128 : 128 + rows, span] = high

        patch = patch_ref[:, own_columns]
        hidden = dot(conv_in_t[...], jnp.concatenate([patch, patch], axis=0))
        queries = dot_columns(scaled_ref[0 : 128 + rows, own_columns], score_w[...])
        high, low = parts_of(queries)
        lefts = [
            jnp.concatenate(
                [high[:, 128 * head : 128 * head + 128], low[:, 128 * head : 128 * head + 128]],
                axis=1,
            )
            for head in range(HEADS)
        ]
        groups = ((0, 2), (2, 4), (4, 5))
        for first, after in groups:
            score_ref[first * width : after * width, :] = dot(
                jnp.concatenate(lefts[first:after], axis=0), scaled_ref[...]
            )
        summed = []
        for first, after in groups:
            for lower in range(first * width, after * width, 32):
                block = score_ref[lower : lower + 32, :]
                peak = jnp.max(block, axis=1, keepdims=True)
                weight_ref[lower : lower + 32, :] = jnp.exp(block - peak).astype(BF16)
            summed.append(
                dot_rows(
                    scaled_ref[rows : 128 + rows, :], weight_ref[first * width : after * width, :]
                )
            )
        summed = jnp.concatenate(summed, axis=1)
        mixed = (summed[0:rows] + summed[128 - rows : 128]) / summed[rows : rows + 1]
        mixed = [mixed[:, width * head : width * (head + 1)] for head in range(HEADS)]
        sent_ref[step] = compact([patch.astype(F32)] + mixed).astype(BF16)
        if comm:
            before = (list(unsent), list(guarded_unsent))
            unsent.clear()
            guarded_unsent.clear()
            groups = [
                tuple(ref.at[step] for ref in (beside_ref, beside_send, beside_recv)),
                tuple(ref.at[step] for ref in (factor_ref, factor_send, factor_recv)),
            ]
            scatter(sent_ref.at[step], *groups[0])
        high, low = parts_of(jnp.concatenate(mixed, axis=0))
        hidden = hidden + dot(mixed_w[...], jnp.concatenate([high, low, high], axis=0))
        factor = lax.rsqrt(jnp.mean(hidden * hidden, axis=0, keepdims=True) + 1e-05)
        factor_sent_ref[step] = jnp.broadcast_to(factor, (8, width))
        if comm:
            scatter(factor_sent_ref.at[step], *groups[1])
        normed = (hidden * factor).astype(BF16)

        projected = dot(temporal_in_t[...], normed).astype(BF16).astype(F32)
        tqueries = projected[:channels] * (1.0 / math.sqrt(head_dim))
        tkv_ref[2 * HALF] = projected[2 * channels :]
        scores = [None] * SPAN

        def score_of(keys):
            return jnp.concatenate(
                [
                    jnp.sum(
                        tqueries[h * head_dim : (h + 1) * head_dim]
                        * keys[h * head_dim : (h + 1) * head_dim],
                        axis=0,
                        keepdims=True,
                    )
                    for h in range(HEADS)
                ],
                axis=0,
            )

        def take(slots):
            for slot in slots:
                part = dot(slot_w[slot], beside_ref[step, slot])
                part = (part * factor_ref[step, slot, 0:1, :]).astype(BF16).astype(F32)
                good = jnp.logical_and(frames[slot] >= 0, frames[slot] <= last_frame)
                scores[slot] = jnp.where(good, score_of(part[:channels]), -jnp.inf)
                tkv_ref[slot] = part[channels:]

        scores[2 * HALF] = score_of(projected[channels : 2 * channels])

        def receive(*slots, groups=groups if comm else ()):
            for slot in slots:
                for group in groups:
                    arrived(slot, *group)

        def pass_on(slot, target, groups=groups[::-1] if comm else ()):
            for group in groups:
                relay(slot, target, *group)

        if step == 0:
            only = [leans] if comm else ()
            receive(0, 1, 2, 3, 4, groups=only)
            pass_on(3 - core, 6, groups=only)
            pass_on(1, 5, groups=only)
            pass_on(0, 7, groups=only)
            shape = (16, common_w.shape[1])
            place = lax.broadcasted_iota(jnp.int32, shape, 1)
            row = lax.broadcasted_iota(jnp.int32, shape, 0)
            spread = jnp.where(place == row + 208, 1.0, 0.0).astype(BF16)

            def weave(slot):
                slot_w[slot] = (
                    common_w[...].astype(F32) + dot_columns(lean_ref[slot], spread)
                ).astype(BF16)

            for slot in (4, 2, 3, 0, 1):
                weave(slot)
            receive(6, 5, 7, groups=only)
            for slot in (6, 5, 7):
                weave(slot)

        def weigh(slots, peak):
            weights = [jnp.exp(scores[slot] - peak) for slot in slots]
            total = functools.reduce(jnp.add, weights)
            rounded = [weight.astype(BF16).astype(F32) for weight in weights]
            mixed = []
            for head in range(HEADS):
                blended = None
                for slot, weight in zip(slots, rounded):
                    term = (
                        weight[head : head + 1]
                        * tkv_ref[slot, head * head_dim : (head + 1) * head_dim, :]
                    )
                    blended = term if blended is None else blended + term
                mixed.append(blended)
            return total, mixed

        if comm:
            after = (list(unsent), list(guarded_unsent))
            unsent[:], guarded_unsent[:] = before
            settle()
            unsent[:], guarded_unsent[:] = after
        receive(4)
        take([4])
        receive(2, 3)
        pass_on(3 - core, 6)
        take([2, 3])
        receive(0)
        pass_on(0, 7)
        receive(1)
        pass_on(1, 5)
        take([0, 1])
        receive(6)
        take([6])
        early = [0, 1, 2, 3, 4, 6, 8]
        early_peak = functools.reduce(jnp.maximum, [scores[slot] for slot in early])
        early_total, early_mixed = weigh(early, early_peak)
        receive(5, 7)
        take([5, 7])
        peak = functools.reduce(jnp.maximum, [early_peak, scores[5], scores[7]])
        late_total, late_mixed = weigh([5, 7], peak)
        shrink = jnp.exp(early_peak - peak)
        total = early_total * shrink + late_total
        mixed = [
            (early_mixed[head] * shrink[head : head + 1] + late_mixed[head])
            / total[head : head + 1]
            for head in range(HEADS)
        ]
        mixed = jnp.concatenate(mixed, axis=0).astype(BF16)
        hidden = hidden + dot(temporal_out_t[...], mixed)
        normed = layer_norm_columns(hidden).astype(BF16)

        taps = dot(conv_out_t[...], normed)
        added = shifted(taps[0:24], 0) + taps[24:48] + shifted(taps[48:72], 2)
        below = push * added[0:8]
        middle = push * added[8:16] + keep * state
        above = push * added[16:24]
        middles.append(middle)
        own_out_ref[step, 0] = below
        own_out_ref[step, 1] = above
        next_out_ref[step, 0:8] = middle
        next_out_ref[step, 8:16] = below + pltpu.roll(above, 4, 0)

        last = step == STEPS - 1
        next_copies = []
        if comm:
            if last:
                ways = [(index, row_at(offset)) for index, offset in enumerate((1, -1, 0))]
            else:
                ways = [(ring * flip + turn, row_by(flip, turn)) for flip, turn in steps]
            for index, target in ways:
                copy = send(
                    next_out_ref.at[step],
                    parts_ref.at[step, me_r],
                    next_send.at[step, index],
                    next_recv.at[step, index],
                    (me_q - 1, target),
                )
                next_copies.append(copy)

            @pl.when(me_q > 0)
            def _():
                for copy in next_copies:
                    copy.start()

            for slot, offset in enumerate((1, -1)):
                copy = send(
                    own_out_ref.at[step, slot],
                    own_in_ref.at[step, slot],
                    own_send.at[step, slot],
                    own_recv.at[step, slot],
                    (me_q, row_at(offset)),
                )
                copy.start()
                own_copies.append(copy)
            if last:
                settle()

            @pl.when(me_q < last_frame)
            def _():
                for copy in next_copies:
                    copy.wait_recv()

            next_sent.append(next_copies)
        entering = me_q == last_frame
        if not last:
            images = []
            for y in range(row_len):
                total = parts_ref[step, y, 0:8]
                if y > 0:
                    total = total + parts_ref[step, y - 1, 8:16]
                if y < row_len - 1:
                    total = total + pltpu.roll(parts_ref[step, y + 1, 8:16], 4, 0)
                total = jnp.where(entering, entered_ref[y], jnp.where(upper, total, 0.0))
                images.append(total)
                frame_ref[y] = total
            state = frame_ref[me_r]
        else:
            total = parts_ref[step, me_r, 0:8]
            total = total + jnp.where(me_r == 0, 0.0, parts_ref[step, row_at(-1), 8:16])
            total = total + jnp.where(
                me_r == row_len - 1, 0.0, pltpu.roll(parts_ref[step, row_at(1), 8:16], 4, 0)
            )
            queue_ref[0, :, 0, :] = jnp.where(entering, noise_ref[step, :, 0, :], total[0:4])

    for copy in own_copies:
        copy.wait()
    for step in range(STEPS):
        total = middles[step]
        total = total + jnp.where(me_r == 0, 0.0, own_in_ref[step, 0])
        total = total + jnp.where(me_r == row_len - 1, 0.0, own_in_ref[step, 1])
        denoised_ref[step, 0, :, 0, :] = total[0:4]
    if comm:
        settle()

        @pl.when(me_q > 0)
        def _():
            for next_copies in next_sent:
                for copy in next_copies:
                    copy.wait_send()


def on_device(
    latents,
    fresh_noise,
    timesteps,
    conv_in_w,
    time_w,
    spatial_in,
    spatial_out,
    temporal_in,
    temporal_out,
    conv_out_w,
    *,
    sizes,
):
    queue_len, row_len, comm = sizes
    channels = conv_in_w.shape[1]
    width = latents.shape[3]
    pixels = row_len * width
    vmem = pl.BlockSpec(memory_space=pltpu.VMEM)
    hbm = pl.BlockSpec(memory_space=pl.ANY)
    dma = pltpu.SemaphoreType.DMA
    weights = (conv_in_w, time_w, spatial_in, spatial_out, temporal_in, temporal_out, conv_out_w.T)
    arguments = (timesteps, latents, fresh_noise) + weights
    return pl.pallas_call(
        functools.partial(kernel, sizes),
        out_shape=(
            jax.ShapeDtypeStruct((STEPS,) + latents.shape, F32),
            jax.ShapeDtypeStruct(latents.shape, F32),
        ),
        in_specs=[hbm] * len(arguments),
        out_specs=(vmem, vmem),
        scratch_shapes=[pltpu.SMEM(timesteps.shape, timesteps.dtype)]
        + [pltpu.VMEM(array.shape, array.dtype) for array in arguments[1:]]
        + [
            pltpu.VMEM((channels, 96), BF16),
            pltpu.VMEM((176, HEADS * 128), BF16),
            pltpu.VMEM((channels, 3 * HEADS * 48), BF16),
            pltpu.VMEM((3 * channels, channels), BF16),
            pltpu.VMEM((channels, channels), BF16),
            pltpu.VMEM((80, channels), BF16),
            pltpu.VMEM((2 * channels, 224), BF16),
            pltpu.VMEM((2 * HALF, 2 * channels, 224), BF16),
            pltpu.VMEM((row_len, 8, width), F32),
            pltpu.VMEM((row_len, 8, width), F32),
            pltpu.VMEM((48, pixels), BF16),
            pltpu.VMEM((256, pixels), BF16),
            pltpu.VMEM((HEADS * width, pixels), F32),
            pltpu.VMEM((HEADS * width, pixels), BF16),
            pltpu.VMEM((SPAN, channels, width), F32),
            pltpu.VMEM((row_len, 8, width), F32),
            pltpu.VMEM((STEPS, 224, width), BF16),
            pltpu.VMEM((STEPS, 2 * HALF, 224, width), BF16),
            pltpu.VMEM((STEPS, 8, width), F32),
            pltpu.VMEM((STEPS, 2 * HALF, 8, width), F32),
            pltpu.VMEM((16, 2 * channels), BF16),
            pltpu.VMEM((2 * HALF, 16, 2 * channels), BF16),
            pltpu.VMEM((224, width), BF16),
            pltpu.VMEM((8, width), F32),
            pltpu.VMEM((16, 2 * channels), BF16),
            pltpu.VMEM((STEPS, row_len, 16, width), F32),
            pltpu.VMEM((STEPS, 2, 8, width), F32),
            pltpu.VMEM((STEPS, 16, width), F32),
            pltpu.VMEM((STEPS, 2, 8, width), F32),
            dma((len(arguments),)),
            dma((row_len,)),
            dma((row_len,)),
            dma((STEPS, 2 * HALF)),
            dma((STEPS, 2 * HALF)),
            dma((STEPS, 2 * HALF)),
            dma((STEPS, 2 * HALF)),
            dma((2 * HALF,)),
            dma((2 * HALF,)),
            dma((STEPS, row_len)),
            dma((STEPS, row_len)),
            dma((STEPS, 2)),
            dma((STEPS, 2)),
        ],
        compiler_params=pltpu.CompilerParams(
            collective_id=0 if comm else None,
            has_side_effects=True,
            vmem_limit_bytes=40 * 1024 * 1024,
        ),
        name="denoise",
    )(*(pltpu.with_memory_space_constraint(array, pltpu.HBM) for array in arguments))


def solution(mesh):
    sizes = (mesh.shape["queue"], mesh.shape["row"], True)
    return jax.shard_map(
        functools.partial(on_device, sizes=sizes),
        mesh=mesh,
        in_specs=(
            P("queue", None, "row", None),
            P(None, None, "row", None),
            P("queue", None),
            P(),
            P(),
            P(),
            P(),
            P(),
            P(),
            P(),
        ),
        out_specs=(P(None, "queue", None, "row", None), P("queue", None, "row", None)),
        check_vma=False,
    )
```
